32 devices in a mesh: grp: 2 (over x), row: 16 (over z, y, core).
Axes of the slice: x: 2, y: 2, z: 4, core: 2. Of those that a mesh axis runs over, the one named last changes fastest.
Arguments:
- pair: bfloat16 [32, 5, 32, 2048], P(('grp', 'row')), parts along dimension 0, may hold values from -6 to 6
- kept: int32 [32, 5], P(('grp', 'row')), parts along dimension 0, may hold values from 0 to 1, as said below
- w_in: bfloat16 [64, 320], replicated, may hold values from -0.75 to 0.75
- w_out: bfloat16 [64, 64], replicated, may hold values from -0.75 to 0.75
- cotangent: bfloat16 [32, 5, 32, 2048], P(('grp', 'row')), parts along dimension 0, may hold values from -6 to 6
Outputs:
- update: bfloat16 [32, 5, 32, 2048], P(('grp', 'row')), parts along dimension 0
- grad_pair: bfloat16 [32, 5, 32, 2048], P(('grp', 'row')), parts along dimension 0
- grad_w_in: float32 [128, 320], P('grp'), parts along dimension 0
- grad_w_out: float32 [128, 64], P('grp'), parts along dimension 0
The draws below stay inside these ranges and needn't reach their ends.
There are 2 independent parts, one for each index of `grp`. The reference program is written for one: setup_inputs(seed, part) draws one part's arguments, and reference() takes and returns one part's arrays. A program takes and returns all parts, laid end to end along the dimension named above; an argument that names none is the same for every part. Nothing has to cross between parts.
Inputs may be any that keep to these rules, and one draw needn't show every extreme that they name: kept[I, 2] is 1 for every block; kept[I, w] is 0 where block I + w - 2 lies outside 0 to 15; the pattern is symmetric: kept[I, w] equals kept[I + w - 2, 4 - w].
All inputs are finite; a program needn't handle non-finite values.
Results may differ from the reference program's by a relative error of at most 0.0086.
Values may be sent and summed in bfloat16 or wider, within the bound.
A program may use at most 128 MiB of HBM per device.

```python
import jax
import jax.numpy as jnp
from jax import lax

C = 64
TILE = 32
BAND = 5
BLOCKS = 16


def draw_kept(key, part):
    key = jax.random.fold_in(key, 7)
    bonds_drawn = (jax.random.randint(key, (BLOCKS, BAND // 2), 0, 5) < 3).astype(jnp.int32)
    positions = jnp.arange(BLOCKS, dtype=jnp.int32)
    half_band = BAND // 2
    column_list = []
    for slot_index in range(BAND):
        offset = slot_index - half_band
        if offset == 0:
            column_list.append(jnp.ones((BLOCKS,), jnp.int32))
        elif offset > 0:
            inside = (positions + offset < BLOCKS).astype(jnp.int32)
            column_list.append(bonds_drawn[:, offset - 1] * inside)
        else:
            inside = (positions + offset >= 0).astype(jnp.int32)
            column_list.append(jnp.roll(bonds_drawn[:, -offset - 1], -offset) * inside)
    return jnp.stack(column_list, axis=1)


def steps_of(stream_key, extent, cuts, smallest, high):
    gain, own = 1.0, jax.random.fold_in(stream_key, 6)
    for dim, parts in cuts:
        draws = jnp.exp(jax.random.uniform(jax.random.fold_in(own, dim), (parts,), jnp.float32, smallest / len(cuts), high / len(cuts)))
        gain = gain * jnp.repeat(draws, extent[dim] // parts).reshape([-1 if axis == dim else 1 for axis in range(len(extent))])
    return gain


def noise(rng, extent, scale, limit, shards=(), kind=jnp.bfloat16):
    values = jax.random.normal(rng, extent, jnp.float32) * scale
    if len(shards) > 0:
        values = steps_of(rng, extent, shards, -0.22, 0.18) * values
    return jnp.clip(values, min=-limit, max=limit).astype(kind)


def setup_inputs(seed: int = 0, part: int = 0) -> dict:
    key_list = jax.random.split(jax.random.key(seed), 6)
    part_splits = jax.random.split(jax.random.fold_in(key_list[5], part), 6)
    pair = noise(part_splits[0], (BLOCKS, BAND, TILE, TILE * C), 1.0, 6.0, ((0, 16),))
    kept = draw_kept(jax.random.fold_in(jax.random.fold_in(key_list[5], part), 71), part)
    w_in = noise(key_list[2], (C, 5 * C), C ** -0.5, 0.75)
    w_out = noise(key_list[3], (C, C), C ** -0.5, 0.75)
    cotangent = noise(part_splits[4], (BLOCKS, BAND, TILE, TILE * C), 1.0, 6.0, ((0, 16),))
    return {"pair": pair, "kept": kept, "w_in": w_in, "w_out": w_out, "cotangent": cotangent}


EPS = 1e-05

def normalize(values):
    average = lax.optimization_barrier(jnp.mean(values, axis=-1, keepdims=True))
    centered = values - average
    variance = lax.optimization_barrier(jnp.mean(centered * centered, axis=-1, keepdims=True))
    return centered * lax.rsqrt(variance + EPS)

def normalize_back(values, incoming):
    average = lax.optimization_barrier(jnp.mean(values, axis=-1, keepdims=True))
    centered = values - average
    variance = lax.optimization_barrier(jnp.mean(centered * centered, axis=-1, keepdims=True))
    scale = lax.rsqrt(variance + EPS)
    normed = centered * scale
    return scale * (incoming - lax.optimization_barrier(jnp.mean(incoming, axis=-1, keepdims=True)) - normed * lax.optimization_barrier(jnp.mean(incoming * normed, axis=-1, keepdims=True)))

def slot_range(offset, band_slots):
    return (max(0, offset), min(band_slots, band_slots + offset))

def project_tiles(pair_tiles, row_mask, w_in):
    channels = w_in.shape[0]
    normed = normalize(pair_tiles.astype(jnp.float32)).astype(jnp.bfloat16)
    projected = jnp.dot(normed.reshape(-1, channels), w_in, preferred_element_type=jnp.float32)
    projected = projected.reshape(pair_tiles.shape[:3] + (5 * channels,))
    gate_a, value_a, gate_b, value_b, gate_g = jnp.split(projected, 5, axis=-1)
    slot_mask = row_mask[:, None, None, None]
    left_tiles = (jax.nn.sigmoid(gate_a) * value_a * slot_mask).astype(jnp.bfloat16)
    right_tiles = (jax.nn.sigmoid(gate_b) * value_b * slot_mask).astype(jnp.bfloat16)
    return (normed, projected, left_tiles, right_tiles, jax.nn.sigmoid(gate_g))

def reference(pair, kept, w_in, w_out, cotangent):
    half_band = BAND // 2
    tiles_all = pair.reshape(BLOCKS, BAND, TILE, TILE, C)
    masks_all = kept.astype(jnp.float32)
    cot_all = cotangent.reshape(BLOCKS, BAND, TILE, TILE, C)

    def first_section(items):
        outputs = project_tiles(items[0], items[1], w_in)
        return (outputs[2], outputs[3])
    left_all, right_all = lax.map(first_section, (tiles_all, masks_all))
    border = jnp.zeros((half_band, BAND, TILE, TILE, C), jnp.bfloat16)
    left_pad = jnp.concatenate([border, left_all, border], axis=0)
    right_pad = jnp.concatenate([border, right_all, border], axis=0)

    def second_section(items):
        block, pair_tiles, row_mask, cot_tiles = items
        normed, projected, left_tiles, right_tiles, gate_values = project_tiles(pair_tiles, row_mask, w_in)
        tri_list = []
        for out_slot in range(BAND):
            offset = out_slot - half_band
            first_slot, end_slot = slot_range(offset, BAND)
            neighbour = lax.dynamic_index_in_dim(right_pad, block + half_band + offset, 0, keepdims=False)
            tri_list.append(jnp.einsum('wikc,wjkc->ijc', left_tiles[first_slot:end_slot].astype(jnp.float32), neighbour[first_slot - offset:end_slot - offset].astype(jnp.float32)))
        triangle = jnp.stack(tri_list)
        tri_normed = normalize(triangle).astype(jnp.bfloat16)
        mixed_out = jnp.dot(tri_normed.reshape(-1, C), w_out, preferred_element_type=jnp.float32).reshape(triangle.shape)
        out_mask = row_mask[:, None, None, None]
        update = (out_mask * gate_values * mixed_out).astype(jnp.bfloat16)
        d_update = cot_tiles.astype(jnp.float32) * out_mask
        d_mixed = (d_update * gate_values).astype(jnp.bfloat16)
        grad_out_local = jnp.dot(tri_normed.reshape(-1, C).T, d_mixed.reshape(-1, C), preferred_element_type=jnp.float32)
        d_tri_normed = jnp.dot(d_mixed.reshape(-1, C), w_out.T, preferred_element_type=jnp.float32).reshape(triangle.shape)
        d_triangle = normalize_back(triangle, d_tri_normed).astype(jnp.bfloat16)
        return (update, d_triangle, grad_out_local)
    blocks_index = jnp.arange(BLOCKS, dtype=jnp.int32)
    update_all, d_tri_all, grad_out_parts = lax.map(second_section, (blocks_index, tiles_all, masks_all, cot_all))
    d_tri_pad = jnp.concatenate([border, d_tri_all, border], axis=0)

    def third_section(items):
        block, pair_tiles, row_mask, cot_tiles, d_triangle = items
        normed, projected, left_tiles, right_tiles, gate_values = project_tiles(pair_tiles, row_mask, w_in)
        d_left = jnp.zeros(pair_tiles.shape, jnp.float32)
        d_right = jnp.zeros(pair_tiles.shape, jnp.float32)
        for out_slot in range(BAND):
            offset = out_slot - half_band
            first_slot, end_slot = slot_range(offset, BAND)
            neighbour = lax.dynamic_index_in_dim(right_pad, block + half_band + offset, 0, keepdims=False)
            left_grad = jnp.einsum('ijc,wjkc->wikc', d_triangle[out_slot].astype(jnp.float32), neighbour[first_slot - offset:end_slot - offset].astype(jnp.float32))
            d_left = d_left.at[first_slot:end_slot].add(left_grad)
            source_grad = lax.dynamic_index_in_dim(d_tri_pad, block + half_band - offset, 0, keepdims=False)
            source_left = lax.dynamic_index_in_dim(left_pad, block + half_band - offset, 0, keepdims=False)
            term = jnp.einsum('ijc,wikc->wjkc', source_grad[out_slot].astype(jnp.float32), source_left[first_slot:end_slot].astype(jnp.float32)).astype(jnp.bfloat16)
            term = lax.optimization_barrier(term).astype(jnp.float32)
            d_right = d_right.at[first_slot - offset:end_slot - offset].add(term)
        slot_mask = row_mask[:, None, None, None]
        d_left = d_left * slot_mask
        d_right = d_right * slot_mask
        d_update = cot_tiles.astype(jnp.float32) * slot_mask
        gate_a, value_a, gate_b, value_b, gate_g = jnp.split(projected, 5, axis=-1)
        tri_list = []
        for out_slot in range(BAND):
            offset = out_slot - half_band
            first_slot, end_slot = slot_range(offset, BAND)
            neighbour = lax.dynamic_index_in_dim(right_pad, block + half_band + offset, 0, keepdims=False)
            tri_list.append(jnp.einsum('wikc,wjkc->ijc', left_tiles[first_slot:end_slot].astype(jnp.float32), neighbour[first_slot - offset:end_slot - offset].astype(jnp.float32)))
        triangle = jnp.stack(tri_list)
        tri_normed = normalize(triangle).astype(jnp.bfloat16)
        mixed_out = jnp.dot(tri_normed.reshape(-1, C), w_out, preferred_element_type=jnp.float32).reshape(triangle.shape)
        d_gate = d_update * mixed_out * gate_values * (1.0 - gate_values)
        sig_a = jax.nn.sigmoid(gate_a)
        sig_b = jax.nn.sigmoid(gate_b)
        d_projected = jnp.concatenate([d_left * value_a * sig_a * (1.0 - sig_a), d_left * sig_a, d_right * value_b * sig_b * (1.0 - sig_b), d_right * sig_b, d_gate], axis=-1).astype(jnp.bfloat16)
        flat_proj = d_projected.reshape(-1, 5 * C)
        grad_in_local = jnp.dot(normed.reshape(-1, C).T, flat_proj, preferred_element_type=jnp.float32)
        d_normed = jnp.dot(flat_proj, w_in.T, preferred_element_type=jnp.float32).reshape(pair_tiles.shape)
        grad_tiles = normalize_back(pair_tiles.astype(jnp.float32), d_normed).astype(jnp.bfloat16)
        return (grad_tiles, grad_in_local)
    grad_pair_all, grad_in_parts = lax.map(third_section, (blocks_index, tiles_all, masks_all, cot_all, d_tri_all))
    return (update_all.reshape(pair.shape), grad_pair_all.reshape(pair.shape), lax.optimization_barrier(jnp.sum(grad_in_parts, axis=0)), lax.optimization_barrier(jnp.sum(grad_out_parts, axis=0)))
```

```python
import functools

import jax
import jax.numpy as jnp
from jax import lax
from jax.experimental import pallas as pl
from jax.experimental.pallas import tpu as pltpu
from jax.sharding import PartitionSpec as P

EPS = 1e-05


def passed_along(x, axis, by):
    devices = lax.axis_size(axis)
    pairs = [(i, i + by) for i in range(devices) if 0 <= i + by < devices]
    return lax.ppermute(x, axis, pairs)


def normalize(values):
    average = jnp.mean(values, axis=-1, keepdims=True)
    centered = values - average
    variance = jnp.mean(centered * centered, axis=-1, keepdims=True)
    return centered * lax.rsqrt(variance + EPS)


def normalize_back(values, incoming):
    average = jnp.mean(values, axis=-1, keepdims=True)
    centered = values - average
    variance = jnp.mean(centered * centered, axis=-1, keepdims=True)
    scale = lax.rsqrt(variance + EPS)
    normed = centered * scale
    return scale * (
        incoming
        - jnp.mean(incoming, axis=-1, keepdims=True)
        - normed * jnp.mean(incoming * normed, axis=-1, keepdims=True)
    )


def row_sum_body(steps, term_ref, total_ref, sent, landed, send_sem, recv_sem):
    me = lax.axis_index("row")
    partners = []
    for step in range(steps):
        bit = 1 << step
        partners.append(me + bit * (1 - 2 * (lax.rem(me // bit, 2))))
    barrier = pltpu.get_barrier_semaphore()
    for partner in partners:
        pl.semaphore_signal(
            barrier, inc=1, device_id={"row": partner}, device_id_type=pl.DeviceIdType.MESH
        )
    pl.semaphore_wait(barrier, steps)
    total = term_ref[...]
    for step, partner in enumerate(partners):
        sent[step] = total
        copy = pltpu.make_async_remote_copy(
            src_ref=sent.at[step],
            dst_ref=landed.at[step],
            send_sem=send_sem.at[step],
            recv_sem=recv_sem.at[step],
            device_id={"row": partner},
            device_id_type=pl.DeviceIdType.MESH,
        )
        copy.start()
        copy.wait()
        total = total + landed[step]
    total_ref[...] = total


def row_sum(term):
    devices = lax.axis_size("row")
    steps = devices.bit_length() - 1
    if steps == 0 or devices != 1 << steps:
        return lax.psum(term, "row")
    whole = pl.BlockSpec(memory_space=pltpu.VMEM)
    return pl.pallas_call(
        functools.partial(row_sum_body, steps),
        out_shape=jax.ShapeDtypeStruct(term.shape, term.dtype),
        in_specs=[whole],
        out_specs=whole,
        scratch_shapes=[
            pltpu.VMEM((steps,) + term.shape, term.dtype),
            pltpu.VMEM((steps,) + term.shape, term.dtype),
            pltpu.SemaphoreType.DMA((steps,)),
            pltpu.SemaphoreType.DMA((steps,)),
        ],
        compiler_params=pltpu.CompilerParams(collective_id=0, has_side_effects=True),
    )(term)


def slot_range(offset, band_slots):
    return (max(0, offset), min(band_slots, band_slots + offset))


def project_tiles(pair_tiles, row_mask, w_in):
    channels = w_in.shape[0]
    normed = normalize(pair_tiles.astype(jnp.float32)).astype(jnp.bfloat16)
    projected = jnp.dot(normed.reshape(-1, channels), w_in, preferred_element_type=jnp.float32)
    projected = projected.reshape(pair_tiles.shape[:3] + (5 * channels,))
    gate_a, value_a, gate_b, value_b, gate_g = jnp.split(projected, 5, axis=-1)
    slot_mask = row_mask[:, None, None, None]
    left_tiles = (jax.nn.sigmoid(gate_a) * value_a * slot_mask).astype(jnp.bfloat16)
    right_tiles = (jax.nn.sigmoid(gate_b) * value_b * slot_mask).astype(jnp.bfloat16)
    return (normed, projected, left_tiles, right_tiles, jax.nn.sigmoid(gate_g))


def outgoing_product(left_part, right_part):
    return jnp.einsum("wcik,wcjk->cij", left_part, right_part, preferred_element_type=jnp.float32)


def back_product(d_tile, left_part, right_part):
    left_grad = jnp.einsum("cij,wcjk->wcik", d_tile, right_part, preferred_element_type=jnp.float32)
    right_term = jnp.einsum("cij,wcik->wcjk", d_tile, left_part, preferred_element_type=jnp.float32)
    return (left_grad, right_term.astype(jnp.bfloat16))


def local(pair, kept, w_in, w_out, cotangent):
    band_slots = pair.shape[1]
    tile_edge = pair.shape[2]
    channels = w_in.shape[0]
    half_band = band_slots // 2
    pair_tiles = pair[0].reshape(band_slots, tile_edge, tile_edge, channels)
    row_mask = kept[0].astype(jnp.float32)
    slot_mask = row_mask[:, None, None, None]
    normed, projected, left_tiles, right_tiles, gate_values = project_tiles(
        pair_tiles, row_mask, w_in
    )
    left_first = jnp.transpose(left_tiles, (0, 3, 1, 2))
    right_first = jnp.transpose(right_tiles, (0, 3, 1, 2))
    first_shape = left_first.shape
    arrived = {}
    for offset in range(-half_band, half_band + 1):
        first_slot, end_slot = slot_range(offset, band_slots)
        if offset == 0:
            arrived[offset] = right_first
        else:
            whole_band = passed_along(right_first, "row", -offset)
            arrived[offset] = whole_band[first_slot - offset : end_slot - offset]
    tri_list = []
    for out_slot in range(band_slots):
        offset = out_slot - half_band
        first_slot, end_slot = slot_range(offset, band_slots)
        left_part = left_first[first_slot:end_slot]
        tri_tile = outgoing_product(left_part, arrived[offset])
        tri_list.append(tri_tile)
    triangle = jnp.transpose(jnp.stack(tri_list), (0, 2, 3, 1))
    tri_normed = normalize(triangle).astype(jnp.bfloat16)
    mixed_out = jnp.dot(
        tri_normed.reshape(-1, channels), w_out, preferred_element_type=jnp.float32
    ).reshape(triangle.shape)
    update = (slot_mask * gate_values * mixed_out).astype(jnp.bfloat16)
    d_update = cotangent[0].reshape(pair_tiles.shape).astype(jnp.float32) * slot_mask
    d_mixed = (d_update * gate_values).astype(jnp.bfloat16)
    d_gate = d_update * mixed_out * gate_values * (1.0 - gate_values)
    grad_out_local = jnp.dot(
        tri_normed.reshape(-1, channels).T,
        d_mixed.reshape(-1, channels),
        preferred_element_type=jnp.float32,
    )
    d_tri_normed = jnp.dot(
        d_mixed.reshape(-1, channels), w_out.T, preferred_element_type=jnp.float32
    ).reshape(triangle.shape)
    d_triangle = normalize_back(triangle, d_tri_normed).astype(jnp.bfloat16)
    d_tri_first = jnp.transpose(d_triangle, (0, 3, 1, 2))
    d_left = jnp.zeros(first_shape, jnp.float32)
    d_right = jnp.zeros(first_shape, jnp.float32)
    for out_slot in range(band_slots):
        offset = out_slot - half_band
        first_slot, end_slot = slot_range(offset, band_slots)
        left_part = left_first[first_slot:end_slot]
        left_grad, right_term = back_product(d_tri_first[out_slot], left_part, arrived[offset])
        d_left = d_left.at[first_slot:end_slot].add(left_grad)
        if offset == 0:
            kept_term = lax.optimization_barrier(right_term).astype(jnp.float32)
            d_right = d_right.at[first_slot:end_slot].add(kept_term)
        else:
            padded = (
                jnp.zeros(first_shape, jnp.bfloat16)
                .at[first_slot - offset : end_slot - offset]
                .set(right_term)
            )
            d_right = d_right + passed_along(padded, "row", offset).astype(jnp.float32)
    d_left = jnp.transpose(d_left, (0, 2, 3, 1)) * slot_mask
    d_right = jnp.transpose(d_right, (0, 2, 3, 1)) * slot_mask
    gate_a, value_a, gate_b, value_b, gate_g = jnp.split(projected, 5, axis=-1)
    sig_a = jax.nn.sigmoid(gate_a)
    sig_b = jax.nn.sigmoid(gate_b)
    d_projected = jnp.concatenate(
        [
            d_left * value_a * sig_a * (1.0 - sig_a),
            d_left * sig_a,
            d_right * value_b * sig_b * (1.0 - sig_b),
            d_right * sig_b,
            d_gate,
        ],
        axis=-1,
    ).astype(jnp.bfloat16)
    flat_proj = d_projected.reshape(-1, 5 * channels)
    grad_in_local = jnp.dot(
        normed.reshape(-1, channels).T, flat_proj, preferred_element_type=jnp.float32
    )
    d_normed = jnp.dot(flat_proj, w_in.T, preferred_element_type=jnp.float32).reshape(
        pair_tiles.shape
    )
    grad_tiles = normalize_back(pair_tiles.astype(jnp.float32), d_normed).astype(jnp.bfloat16)
    summed = row_sum(jnp.concatenate([grad_in_local, grad_out_local], axis=1))
    grad_w_in, grad_w_out = (summed[:, : 5 * channels], summed[:, 5 * channels :])
    return (update.reshape(pair.shape), grad_tiles.reshape(pair.shape), grad_w_in, grad_w_out)


def solution(mesh):
    return jax.shard_map(
        local,
        mesh=mesh,
        in_specs=(
            P(("grp", "row"), None, None, None),
            P(("grp", "row"), None),
            P(),
            P(),
            P(("grp", "row"), None, None, None),
        ),
        out_specs=(
            P(("grp", "row"), None, None, None),
            P(("grp", "row"), None, None, None),
            P("grp", None),
            P("grp", None),
        ),
        check_vma=False,
    )
```

```python
import functools

import jax
import jax.numpy as jnp
from jax import lax
from jax.experimental import pallas as pl
from jax.experimental.pallas import tpu as pltpu
from jax.sharding import PartitionSpec as P

EPS = 1e-05
F32 = jnp.float32
BF16 = jnp.bfloat16
NN = (((1,), (0,)), ((), ()))
NT = (((1,), (1,)), ((), ()))
TN = (((0,), (0,)), ((), ()))


def dot(a, b, dims):
    return lax.dot_general(a, b, dims, preferred_element_type=F32)


def unit(values):
    average = jnp.mean(values, axis=0, keepdims=True)
    centered = values - average
    variance = jnp.mean(centered * centered, axis=0, keepdims=True)
    scale = lax.rsqrt(variance + EPS)
    return centered * scale, scale


def unit_back(normed, scale, incoming):
    return scale * (
        incoming
        - jnp.mean(incoming, axis=0, keepdims=True)
        - normed * jnp.mean(incoming * normed, axis=0, keepdims=True)
    )


def gated(projected, channels, group):
    gate = jax.nn.sigmoid(projected[2 * group * channels : (2 * group + 1) * channels])
    return gate * projected[(2 * group + 1) * channels : (2 * group + 2) * channels]


def taken(ref, rows, wide, *first):
    lanes = ref.shape[-1]
    chunks = [ref[(*first, k, rows, slice(None))] for k in range(ref.shape[-3])]
    return jnp.concatenate(chunks, axis=1)[:, :wide] if len(chunks) * lanes > wide else chunks[0]


def put(ref, rows, values, *first):
    lanes = ref.shape[-1]
    short = ref.shape[-3] * lanes - values.shape[1]
    if short > 0:
        values = jnp.concatenate([values, jnp.zeros((values.shape[0], short), F32)], axis=1)
    for k in range(ref.shape[-3]):
        ref[(*first, k, rows, slice(None))] = values[:, k * lanes : (k + 1) * lanes]


def body(
    devices,
    slots,
    edge,
    channels,
    own_ref, s0, s1, s2, s3, cot_ref, mask_ref, w_in_ref, w_in_t_ref, w_out_ref, w_out_t_ref,
    update_ref, grad_ref, weights_ref,
    slabs, left, right, band, gates, d_gates, tri, d_left, d_right, packed, arrived, spread,
    terms, landed, slab_send, slab_recv, pack_send, pack_recv, sum_send, sum_recv,
):
    half = slots // 2
    rows = edge * channels
    wide = slots * edge
    lanes = slabs.shape[2]
    folds = lanes // edge
    steps = devices.bit_length() - 1
    offsets = [d for d in range(-half, half + 1) if d != 0]
    slab_refs = dict(zip(offsets, (s0, s1, s2, s3)))
    me = lax.axis_index("row")

    def there(d):
        return jnp.logical_and(me + d >= 0, me + d < devices)

    partners = []
    for step in range(steps):
        bit = 1 << step
        partners.append(me + bit * (1 - 2 * lax.rem(me // bit, 2)))

    def greet(target):
        pl.semaphore_signal(
            barrier, inc=1, device_id={"row": target}, device_id_type=pl.DeviceIdType.MESH
        )

    barrier = pltpu.get_barrier_semaphore()
    for d in offsets:
        pl.when(there(d))(functools.partial(greet, me + d))
    for partner in partners:
        greet(partner)
    pl.semaphore_wait(barrier, steps + sum(there(d).astype(jnp.int32) for d in offsets))

    def slab_copy(d):
        return pltpu.make_async_remote_copy(
            src_ref=slab_refs[d],
            dst_ref=slabs.at[offsets.index(-d)],
            send_sem=slab_send.at[offsets.index(d)],
            recv_sem=slab_recv.at[offsets.index(-d)],
            device_id={"row": me + d},
            device_id_type=pl.DeviceIdType.MESH,
        )

    def slab_arrival(d):
        return pltpu.make_async_remote_copy(
            src_ref=slab_refs[d],
            dst_ref=slabs.at[offsets.index(d)],
            send_sem=slab_send.at[offsets.index(d)],
            recv_sem=slab_recv.at[offsets.index(d)],
            device_id={"row": me + d},
            device_id_type=pl.DeviceIdType.MESH,
        )

    def pack_copy(d, landing):
        return pltpu.make_async_remote_copy(
            src_ref=packed.at[offsets.index(d)],
            dst_ref=arrived.at[offsets.index(landing)],
            send_sem=pack_send.at[offsets.index(d)],
            recv_sem=pack_recv.at[offsets.index(landing)],
            device_id={"row": me + d},
            device_id_type=pl.DeviceIdType.MESH,
        )

    for d in offsets:
        pl.when(there(d))(lambda d=d: slab_copy(d).start())

    w_in = w_in_ref[...]
    w_in_t = w_in_t_ref[...]
    w_out = w_out_ref[...]
    w_out_t = w_out_t_ref[...]
    mask = mask_ref[...]

    def at(i):
        return pl.ds(pl.multiple_of(i * channels, channels), channels)

    def project_own(i, carry):
        normed, _ = unit(own_ref[at(i), :].astype(F32))
        projected = dot(w_in_t, normed.astype(BF16), NN)
        put(left, at(i), gated(projected, channels, 0).astype(BF16).astype(F32), half)
        put(right, at(i), gated(projected, channels, 1).astype(BF16).astype(F32), half)
        gates[at(i), :] = jax.nn.sigmoid(projected[4 * channels :])
        return carry

    lax.fori_loop(0, edge, project_own, 0)

    for d in offsets:
        index = offsets.index(d)
        count = slots - abs(d)
        first = max(0, d) * edge

        def absent(index=index):
            slabs[index] = jnp.zeros((rows, lanes), BF16)

        pl.when(there(d))(lambda d=d: slab_arrival(d).wait_recv())
        pl.when(jnp.logical_not(there(d)))(absent)

        def placed(values, first=first, count=count):
            values = values[:, : count * edge]
            parts = [values]
            if first > 0:
                parts = [jnp.zeros((channels, first), F32)] + parts
            tail = wide - first - count * edge
            if tail > 0:
                parts = parts + [jnp.zeros((channels, tail), F32)]
            return jnp.concatenate(parts, axis=1)

        def project_far(i, carry, d=d, index=index, placed=placed):
            normed, _ = unit(slabs[index, at(i), :].astype(F32))
            projected = dot(w_in_t[: 4 * channels], normed.astype(BF16), NN)
            for group, ref in enumerate((left, right)):
                values = placed(gated(projected, channels, group)).astype(BF16).astype(F32)
                put(ref, at(i), values, half + d)
            return carry

        lax.fori_loop(0, edge, project_far, 0)

    def triangle(c, carry):
        every = pl.ds(c, edge, stride=channels)
        block = jnp.concatenate([taken(right, every, wide, v) for v in range(slots)], axis=0).astype(BF16)
        band[c] = block
        put(tri, every, dot(taken(left, every, wide, half).astype(BF16), block, NT))
        return carry

    lax.fori_loop(0, channels, triangle, 0)

    def middle(start, carry):
        total = carry
        d_tiles = []
        for fold in range(folds):
            i = start + fold * (edge // folds)
            normed, scale = unit(taken(tri, at(i), wide))
            normed_low = normed.astype(BF16)
            mixed = dot(w_out_t, normed_low, NN)
            gate = gates[at(i), :]
            update_ref[at(i), :] = (mask * gate * mixed).astype(BF16)
            d_update = cot_ref[at(i), :].astype(F32) * mask
            d_mixed = (d_update * gate).astype(BF16)
            d_gates[at(i), :] = d_update * mixed * gate * (1.0 - gate)
            total = total + dot(normed_low, d_mixed, NT)
            d_tri = unit_back(normed, scale, dot(w_out, d_mixed, NN)).astype(BF16).astype(F32)
            put(tri, at(i), d_tri)
            d_tiles.append(d_tri)
        for d in offsets:
            v = half + d
            packed[offsets.index(d), at(start), :] = jnp.concatenate(
                [tile[:, v * edge : (v + 1) * edge] for tile in d_tiles], axis=1
            ).astype(BF16)
        return total

    grad_out = lax.fori_loop(0, edge // folds, middle, jnp.zeros((channels, channels), F32))

    for d in offsets:
        pl.when(there(d))(lambda d=d: pack_copy(d, -d).start())

    def to_left(c, carry):
        every = pl.ds(c, edge, stride=channels)
        put(d_left, every, dot(taken(tri, every, wide).astype(BF16), band[c], NN))
        return carry

    lax.fori_loop(0, channels, to_left, 0)

    for d in offsets:
        index = offsets.index(d)

        def absent(index=index):
            arrived[index] = jnp.zeros(arrived.shape[1:], BF16)

        pl.when(there(d))(lambda d=d: pack_copy(d, d).wait_recv())
        pl.when(jnp.logical_not(there(d)))(absent)
        spread[index] = arrived[index].astype(F32)

    def to_right(c, carry):
        every = pl.ds(c, edge, stride=channels)
        folded = pl.ds(c, edge // folds, stride=channels)
        pieces = []
        sources = []
        for d in range(-half, half + 1):
            sources.append(taken(left, every, wide, half + d))
            if d == 0:
                pieces.append(taken(tri, every, wide)[:, half * edge : (half + 1) * edge])
            else:
                tile = spread[offsets.index(d), folded, :]
                for fold in range(folds):
                    pieces.append(tile[:, fold * edge : (fold + 1) * edge])
        d_tile = jnp.concatenate(pieces, axis=0).astype(BF16)
        source = jnp.concatenate(sources, axis=0).astype(BF16)
        put(d_right, every, dot(d_tile, source, TN))
        return carry

    lax.fori_loop(0, channels, to_right, 0)

    def last(i, carry):
        normed, scale = unit(own_ref[at(i), :].astype(F32))
        normed_low = normed.astype(BF16)
        projected = dot(w_in_t[: 4 * channels], normed_low, NN)
        parts = []
        for group, ref in enumerate((d_left, d_right)):
            gate = jax.nn.sigmoid(projected[2 * group * channels : (2 * group + 1) * channels])
            value = projected[(2 * group + 1) * channels : (2 * group + 2) * channels]
            to_value = taken(ref, at(i), wide) * mask * gate
            parts.append(to_value * value * (1.0 - gate))
            parts.append(to_value)
        parts.append(d_gates[at(i), :])
        d_projected = jnp.concatenate(parts, axis=0).astype(BF16)
        grad_ref[at(i), :] = unit_back(normed, scale, dot(w_in, d_projected, NN)).astype(BF16)
        return carry + dot(d_projected, normed_low, NT)

    grad_in = lax.fori_loop(0, edge, last, jnp.zeros((5 * channels, channels), F32))

    total = jnp.concatenate([grad_in, grad_out], axis=0)
    for step, partner in enumerate(partners):
        terms[step] = total
        copy = pltpu.make_async_remote_copy(
            src_ref=terms.at[step],
            dst_ref=landed.at[step],
            send_sem=sum_send.at[step],
            recv_sem=sum_recv.at[step],
            device_id={"row": partner},
            device_id_type=pl.DeviceIdType.MESH,
        )
        copy.start()
        copy.wait()
        total = total + landed[step]
    weights_ref[...] = total

    for d in offsets:
        pl.when(there(d))(lambda d=d: slab_copy(d).wait_send())
        pl.when(there(d))(lambda d=d: pack_copy(d, -d).wait_send())


def local(pair, kept, w_in, w_out, cotangent):
    slots, edge = pair.shape[1], pair.shape[2]
    channels = w_in.shape[0]
    half = slots // 2
    rows, wide = edge * channels, slots * edge
    lanes = 128
    chunks = -(-wide // lanes)
    devices = lax.axis_size("row")
    steps = devices.bit_length() - 1

    def to_columns(tiles):
        return jnp.transpose(tiles, (1, 3, 0, 2)).reshape(rows, wide)

    def from_columns(columns):
        tiles = columns.reshape(edge, channels, slots, edge)
        return jnp.transpose(tiles, (2, 0, 3, 1)).reshape(pair.shape)

    tiles = pair[0].reshape(slots, edge, edge, channels)
    own = to_columns(tiles * kept[0].astype(BF16)[:, None, None, None])
    cot = to_columns(cotangent[0].reshape(tiles.shape))
    mask = jnp.repeat(kept[0].astype(F32), edge)[None, :]
    slabs = []
    for d in range(-half, half + 1):
        if d != 0:
            low = max(0, d) * edge
            count = (slots - abs(d)) * edge
            slab = own[:, low : low + count]
            slabs.append(jnp.pad(slab, ((0, 0), (0, lanes - count))))

    whole = pl.BlockSpec(memory_space=pltpu.VMEM)
    far = len(slabs)
    update, grad, weights = pl.pallas_call(
        functools.partial(body, devices, slots, edge, channels),
        out_shape=(
            jax.ShapeDtypeStruct((rows, wide), BF16),
            jax.ShapeDtypeStruct((rows, wide), BF16),
            jax.ShapeDtypeStruct((6 * channels, channels), F32),
        ),
        in_specs=[whole] * 11,
        out_specs=(whole, whole, whole),
        scratch_shapes=[
            pltpu.VMEM((far, rows, lanes), BF16),
            pltpu.VMEM((slots, chunks, rows, lanes), F32),
            pltpu.VMEM((slots, chunks, rows, lanes), F32),
            pltpu.VMEM((channels, wide, wide), BF16),
            pltpu.VMEM((rows, wide), F32),
            pltpu.VMEM((rows, wide), F32),
            pltpu.VMEM((chunks, rows, lanes), F32),
            pltpu.VMEM((chunks, rows, lanes), F32),
            pltpu.VMEM((chunks, rows, lanes), F32),
            pltpu.VMEM((far, rows * edge // lanes, lanes), BF16),
            pltpu.VMEM((far, rows * edge // lanes, lanes), BF16),
            pltpu.VMEM((far, rows * edge // lanes, lanes), F32),
            pltpu.VMEM((steps, 6 * channels, channels), F32),
            pltpu.VMEM((steps, 6 * channels, channels), F32),
            pltpu.SemaphoreType.DMA((far,)),
            pltpu.SemaphoreType.DMA((far,)),
            pltpu.SemaphoreType.DMA((far,)),
            pltpu.SemaphoreType.DMA((far,)),
            pltpu.SemaphoreType.DMA((steps,)),
            pltpu.SemaphoreType.DMA((steps,)),
        ],
        compiler_params=pltpu.CompilerParams(
            collective_id=0, has_side_effects=True, vmem_limit_bytes=60 * 1024 * 1024
        ),
    )(own, *slabs, cot, mask, w_in, w_in.T, w_out, w_out.T)
    grad_w_in = weights[: 5 * channels].T
    grad_w_out = weights[5 * channels :]
    return (from_columns(update), from_columns(grad), grad_w_in, grad_w_out)


def solution(mesh):
    tiled = P(("grp", "row"), None, None, None)
    return jax.shard_map(
        local,
        mesh=mesh,
        in_specs=(tiled, P(("grp", "row"), None), P(), P(), tiled),
        out_specs=(tiled, tiled, P("grp", None), P("grp", None)),
        check_vma=False,
    )
```

```python
import functools

import jax
import jax.numpy as jnp
from jax import lax
from jax.experimental import pallas as pl
from jax.experimental.pallas import tpu as pltpu
from jax.sharding import PartitionSpec as P

EPS = 1e-05
F32 = jnp.float32
BF16 = jnp.bfloat16
NN = (((1,), (0,)), ((), ()))
NT = (((1,), (1,)), ((), ()))
TN = (((0,), (0,)), ((), ()))


def dot(a, b, dims):
    return lax.dot_general(a, b, dims, preferred_element_type=F32)


def unit(values):
    average = jnp.mean(values, axis=0, keepdims=True)
    centered = values - average
    variance = jnp.mean(centered * centered, axis=0, keepdims=True)
    scale = lax.rsqrt(variance + EPS)
    return centered * scale, scale


def unit_back(normed, scale, incoming):
    return scale * (
        incoming
        - jnp.mean(incoming, axis=0, keepdims=True)
        - normed * jnp.mean(incoming * normed, axis=0, keepdims=True)
    )


def gated(projected, channels, group):
    gate = jax.nn.sigmoid(projected[2 * group * channels : (2 * group + 1) * channels])
    return gate * projected[(2 * group + 1) * channels : (2 * group + 2) * channels]


def taken(ref, rows, wide, *first):
    lanes = ref.shape[-1]
    chunks = [ref[(*first, k, rows, slice(None))] for k in range(ref.shape[-3])]
    return jnp.concatenate(chunks, axis=1)[:, :wide] if len(chunks) * lanes > wide else chunks[0]


def put(ref, rows, values, *first):
    lanes = ref.shape[-1]
    short = ref.shape[-3] * lanes - values.shape[1]
    if short > 0:
        values = jnp.concatenate([values, jnp.zeros((values.shape[0], short), F32)], axis=1)
    for k in range(ref.shape[-3]):
        ref[(*first, k, rows, slice(None))] = values[:, k * lanes : (k + 1) * lanes]


def looped(first, end, batch, compute):
    def step(block, carry):
        stores = [compute(block * batch + k) for k in range(batch)]
        for store in stores:
            store()
        return carry

    lax.fori_loop(first // batch, end // batch, step, 0)


def body(
    devices,
    slots,
    edge,
    channels,
    own_ref, s0, s1, s2, s3, cot_ref, mask_ref, w_in_ref, w_in_t_ref, w_out_ref, w_out_t_ref,
    update_ref, grad_ref, weights_ref,
    slabs, left, right, band, gates, saved, d_projected, tri, d_left, d_right, packed, arrived, spread,
    terms, landed, slab_send, slab_recv, pack_send, pack_recv, sum_send, sum_recv,
):
    half = slots // 2
    rows = edge * channels
    wide = slots * edge
    lanes = slabs.shape[2]
    folds = lanes // edge
    steps = devices.bit_length() - 1
    offsets = [d for d in range(-half, half + 1) if d != 0]
    slab_refs = dict(zip(offsets, (s0, s1, s2, s3)))
    me = lax.axis_index("row")

    def there(d):
        return jnp.logical_and(me + d >= 0, me + d < devices)

    partners = []
    for step in range(steps):
        bit = 1 << step
        partners.append(me + bit * (1 - 2 * lax.rem(me // bit, 2)))

    def greet(target):
        pl.semaphore_signal(
            barrier, inc=1, device_id={"row": target}, device_id_type=pl.DeviceIdType.MESH
        )

    barrier = pltpu.get_barrier_semaphore()
    for d in offsets:
        pl.when(there(d))(functools.partial(greet, me + d))
    for partner in partners:
        greet(partner)
    pl.semaphore_wait(barrier, steps + sum(there(d).astype(jnp.int32) for d in offsets))

    def slab_copy(d):
        return pltpu.make_async_remote_copy(
            src_ref=slab_refs[d],
            dst_ref=slabs.at[offsets.index(-d)],
            send_sem=slab_send.at[offsets.index(d)],
            recv_sem=slab_recv.at[offsets.index(-d)],
            device_id={"row": me + d},
            device_id_type=pl.DeviceIdType.MESH,
        )

    def slab_arrival(d):
        return pltpu.make_async_remote_copy(
            src_ref=slab_refs[d],
            dst_ref=slabs.at[offsets.index(d)],
            send_sem=slab_send.at[offsets.index(d)],
            recv_sem=slab_recv.at[offsets.index(d)],
            device_id={"row": me + d},
            device_id_type=pl.DeviceIdType.MESH,
        )

    def pack_copy(d, landing):
        return pltpu.make_async_remote_copy(
            src_ref=packed.at[offsets.index(d)],
            dst_ref=arrived.at[offsets.index(landing)],
            send_sem=pack_send.at[offsets.index(d)],
            recv_sem=pack_recv.at[offsets.index(landing)],
            device_id={"row": me + d},
            device_id_type=pl.DeviceIdType.MESH,
        )

    for d in offsets:
        pl.when(there(d))(lambda d=d: slab_copy(d).start())

    w_in = w_in_ref[...]
    w_in_t = w_in_t_ref[...]
    w_out = w_out_ref[...]
    w_out_t = w_out_t_ref[...]
    mask = mask_ref[...]

    def at(i):
        return pl.ds(pl.multiple_of(i * channels, channels), channels)

    def four(i):
        return pl.ds(pl.multiple_of(i * 4 * channels, channels), 4 * channels)

    def project_own(i):
        normed, _ = unit(own_ref[at(i), :].astype(F32))
        projected = dot(w_in_t, normed.astype(BF16), NN)
        parts = []
        for group in range(2):
            low = 2 * group * channels
            parts.append(jax.nn.sigmoid(projected[low : low + channels]))
            parts.append(projected[low + channels : low + 2 * channels])
        gate = jax.nn.sigmoid(projected[4 * channels :])

        def store():
            put(left, at(i), (parts[0] * parts[1]).astype(BF16).astype(F32), half)
            put(right, at(i), (parts[2] * parts[3]).astype(BF16).astype(F32), half)
            saved[four(i), :] = jnp.concatenate(parts, axis=0)
            gates[at(i), :] = gate

        return store

    looped(0, edge, 2, project_own)

    for d in sorted(offsets, key=abs):
        index = offsets.index(d)
        count = slots - abs(d)
        first = max(0, d) * edge

        def absent(index=index):
            slabs[index] = jnp.zeros((rows, lanes), BF16)

        pl.when(there(d))(lambda d=d: slab_arrival(d).wait_recv())
        pl.when(jnp.logical_not(there(d)))(absent)

        def placed(values, first=first, count=count):
            values = values[:, : count * edge]
            parts = [values]
            if first > 0:
                parts = [jnp.zeros((channels, first), F32)] + parts
            tail = wide - first - count * edge
            if tail > 0:
                parts = parts + [jnp.zeros((channels, tail), F32)]
            return jnp.concatenate(parts, axis=1)

        def project_far(block, d=d, index=index, placed=placed):
            picked = [block * 4 + k for k in range(4)]
            values = jnp.concatenate([slabs[index, at(i), :] for i in picked], axis=1)
            normed, _ = unit(values.astype(F32))
            projected = dot(w_in_t[: 4 * channels], normed.astype(BF16), NN)
            results = [gated(projected, channels, group).astype(BF16).astype(F32) for group in range(2)]

            def store():
                for result, ref in zip(results, (left, right)):
                    for k, i in enumerate(picked):
                        put(ref, at(i), placed(result[:, k * lanes : (k + 1) * lanes]), half + d)

            return store

        looped(0, edge // 4, 1, project_far)

    def triangle(c):
        every = pl.ds(c, edge, stride=channels)
        block = jnp.concatenate([taken(right, every, wide, v) for v in range(slots)], axis=0).astype(BF16)
        result = dot(taken(left, every, wide, half).astype(BF16), block, NT)

        def store():
            band[c] = block
            put(tri, every, result)

        return store

    looped(0, channels, 4, triangle)

    def middle(start, carry):
        total = carry
        d_tiles = []
        for fold in range(folds):
            i = start + fold * (edge // folds)
            normed, scale = unit(taken(tri, at(i), wide))
            normed_low = normed.astype(BF16)
            mixed = dot(w_out_t, normed_low, NN)
            gate = gates[at(i), :]
            update_ref[at(i), :] = (mask * gate * mixed).astype(BF16)
            d_update = cot_ref[at(i), :].astype(F32) * mask
            d_mixed = (d_update * gate).astype(BF16)
            d_projected[i, 4 * channels :, :] = (d_update * mixed * gate * (1.0 - gate)).astype(BF16)
            total = total + dot(normed_low, d_mixed, NT)
            d_tri = unit_back(normed, scale, dot(w_out, d_mixed, NN)).astype(BF16).astype(F32)
            put(tri, at(i), d_tri)
            d_tiles.append(d_tri)
        for d in offsets:
            v = half + d
            packed[offsets.index(d), at(start), :] = jnp.concatenate(
                [tile[:, v * edge : (v + 1) * edge] for tile in d_tiles], axis=1
            ).astype(BF16)
        return total

    grad_out = lax.fori_loop(0, edge // folds, middle, jnp.zeros((channels, channels), F32))

    for d in offsets:
        pl.when(there(d))(lambda d=d: pack_copy(d, -d).start())

    def to_left(c):
        every = pl.ds(c, edge, stride=channels)
        result = dot(taken(tri, every, wide).astype(BF16), band[c], NN)
        return lambda: put(d_left, every, result)

    looped(0, channels, 4, to_left)

    for d in offsets:
        index = offsets.index(d)

        def absent(index=index):
            arrived[index] = jnp.zeros(arrived.shape[1:], BF16)

        pl.when(there(d))(lambda d=d: pack_copy(d, d).wait_recv())
        pl.when(jnp.logical_not(there(d)))(absent)
        spread[index] = arrived[index].astype(F32)

    def to_right(c):
        every = pl.ds(c, edge, stride=channels)
        folded = pl.ds(c, edge // folds, stride=channels)
        pieces = []
        sources = []
        for d in range(-half, half + 1):
            sources.append(taken(left, every, wide, half + d))
            if d == 0:
                pieces.append(taken(tri, every, wide)[:, half * edge : (half + 1) * edge])
            else:
                tile = spread[offsets.index(d), folded, :]
                for fold in range(folds):
                    pieces.append(tile[:, fold * edge : (fold + 1) * edge])
        d_tile = jnp.concatenate(pieces, axis=0).astype(BF16)
        source = jnp.concatenate(sources, axis=0).astype(BF16)
        result = dot(d_tile, source, TN)
        return lambda: put(d_right, every, result)

    looped(0, channels, 4, to_right)

    def last(block, carry):
        stores = []
        for i in (2 * block, 2 * block + 1):
            normed, _ = unit(own_ref[at(i), :].astype(F32))
            held = saved[four(i), :]
            parts = []
            for group, ref in enumerate((d_left, d_right)):
                gate = held[2 * group * channels : (2 * group + 1) * channels]
                value = held[(2 * group + 1) * channels : (2 * group + 2) * channels]
                to_value = taken(ref, at(i), wide) * mask * gate
                parts.append((to_value * value * (1.0 - gate)).astype(BF16))
                parts.append(to_value.astype(BF16))
            front = jnp.concatenate(parts, axis=0)
            stores.append((i, front))
            joined = jnp.concatenate([front, d_projected[i, 4 * channels :, :]], axis=0)
            carry = carry + dot(normed.astype(BF16), joined, NT)
        for i, front in stores:
            d_projected[i, : 4 * channels, :] = front
        return carry

    grad_in = lax.fori_loop(0, edge // 2, last, jnp.zeros((channels, 5 * channels), F32))

    def to_pair(i):
        normed, scale = unit(own_ref[at(i), :].astype(F32))
        result = unit_back(normed, scale, dot(w_in, d_projected[i], NN)).astype(BF16)

        def store():
            grad_ref[at(i), :] = result

        return store

    total = jnp.concatenate([grad_in, grad_out], axis=1)
    for step, partner in enumerate(partners):
        terms[step] = total
        copy = pltpu.make_async_remote_copy(
            src_ref=terms.at[step],
            dst_ref=landed.at[step],
            send_sem=sum_send.at[step],
            recv_sem=sum_recv.at[step],
            device_id={"row": partner},
            device_id_type=pl.DeviceIdType.MESH,
        )
        copy.start()
        looped(edge // 2 * step // steps * 2, edge // 2 * (step + 1) // steps * 2, 2, to_pair)
        copy.wait()
        total = total + landed[step]
    weights_ref[...] = total

    for d in offsets:
        pl.when(there(d))(lambda d=d: slab_copy(d).wait_send())
        pl.when(there(d))(lambda d=d: pack_copy(d, -d).wait_send())


def local(pair, kept, w_in, w_out, cotangent):
    slots, edge = pair.shape[1], pair.shape[2]
    channels = w_in.shape[0]
    half = slots // 2
    rows, wide = edge * channels, slots * edge
    lanes = 128
    chunks = -(-wide // lanes)
    devices = lax.axis_size("row")
    steps = devices.bit_length() - 1

    def to_columns(tiles):
        return jnp.transpose(tiles, (1, 3, 0, 2)).reshape(rows, wide)

    def from_columns(columns):
        tiles = columns.reshape(edge, channels, slots, edge)
        return jnp.transpose(tiles, (2, 0, 3, 1)).reshape(pair.shape)

    tiles = pair[0].reshape(slots, edge, edge, channels)
    own = to_columns(tiles * kept[0].astype(BF16)[:, None, None, None])
    cot = to_columns(cotangent[0].reshape(tiles.shape))
    mask = jnp.repeat(kept[0].astype(F32), edge)[None, :]
    slabs = []
    for d in range(-half, half + 1):
        if d != 0:
            low = max(0, d) * edge
            count = (slots - abs(d)) * edge
            slab = own[:, low : low + count]
            slabs.append(jnp.pad(slab, ((0, 0), (0, lanes - count))))

    whole = pl.BlockSpec(memory_space=pltpu.VMEM)
    far = len(slabs)
    update, grad, weights = pl.pallas_call(
        functools.partial(body, devices, slots, edge, channels),
        out_shape=(
            jax.ShapeDtypeStruct((rows, wide), BF16),
            jax.ShapeDtypeStruct((rows, wide), BF16),
            jax.ShapeDtypeStruct((channels, 6 * channels), F32),
        ),
        in_specs=[whole] * 11,
        out_specs=(whole, whole, whole),
        scratch_shapes=[
            pltpu.VMEM((far, rows, lanes), BF16),
            pltpu.VMEM((slots, chunks, rows, lanes), F32),
            pltpu.VMEM((slots, chunks, rows, lanes), F32),
            pltpu.VMEM((channels, wide, wide), BF16),
            pltpu.VMEM((rows, wide), F32),
            pltpu.VMEM((4 * rows, wide), F32),
            pltpu.VMEM((edge, 5 * channels, wide), BF16),
            pltpu.VMEM((chunks, rows, lanes), F32),
            pltpu.VMEM((chunks, rows, lanes), F32),
            pltpu.VMEM((chunks, rows, lanes), F32),
            pltpu.VMEM((far, rows * edge // lanes, lanes), BF16),
            pltpu.VMEM((far, rows * edge // lanes, lanes), BF16),
            pltpu.VMEM((far, rows * edge // lanes, lanes), F32),
            pltpu.VMEM((steps, channels, 6 * channels), F32),
            pltpu.VMEM((steps, channels, 6 * channels), F32),
            pltpu.SemaphoreType.DMA((far,)),
            pltpu.SemaphoreType.DMA((far,)),
            pltpu.SemaphoreType.DMA((far,)),
            pltpu.SemaphoreType.DMA((far,)),
            pltpu.SemaphoreType.DMA((steps,)),
            pltpu.SemaphoreType.DMA((steps,)),
        ],
        compiler_params=pltpu.CompilerParams(
            collective_id=0, has_side_effects=True, vmem_limit_bytes=63 * 1024 * 1024
        ),
    )(own, *slabs, cot, mask, w_in, w_in.T, w_out, w_out.T)
    grad_w_in = weights[:, : 5 * channels]
    grad_w_out = weights[:, 5 * channels :]
    return (from_columns(update), from_columns(grad), grad_w_in, grad_w_out)


def solution(mesh):
    tiled = P(("grp", "row"), None, None, None)
    return jax.shard_map(
        local,
        mesh=mesh,
        in_specs=(tiled, P(("grp", "row"), None), P(), P(), tiled),
        out_specs=(tiled, tiled, P("grp", None), P("grp", None)),
        check_vma=False,
    )
```

```python
import functools

import jax
import jax.numpy as jnp
from jax import lax
from jax.experimental import pallas as pl
from jax.experimental.pallas import tpu as pltpu
from jax.sharding import PartitionSpec as P

EPS = 1e-05
F32 = jnp.float32
BF16 = jnp.bfloat16
NN = (((1,), (0,)), ((), ()))
NT = (((1,), (1,)), ((), ()))
TN = (((0,), (0,)), ((), ()))


def dot(a, b, dims):
    return lax.dot_general(a, b, dims, preferred_element_type=F32)


def unit(values):
    average = jnp.mean(values, axis=0, keepdims=True)
    centered = values - average
    variance = jnp.mean(centered * centered, axis=0, keepdims=True)
    scale = lax.rsqrt(variance + EPS)
    return centered * scale, scale


def unit_back(normed, scale, incoming):
    return scale * (
        incoming
        - jnp.mean(incoming, axis=0, keepdims=True)
        - normed * jnp.mean(incoming * normed, axis=0, keepdims=True)
    )


def gated(projected, channels, group):
    gate = jax.nn.sigmoid(projected[2 * group * channels : (2 * group + 1) * channels])
    return gate * projected[(2 * group + 1) * channels : (2 * group + 2) * channels]


def taken(ref, rows, wide, *first):
    lanes = ref.shape[-1]
    chunks = [ref[(*first, k, rows, slice(None))] for k in range(ref.shape[-3])]
    return jnp.concatenate(chunks, axis=1)[:, :wide] if len(chunks) * lanes > wide else chunks[0]


def put(ref, rows, values, *first):
    lanes = ref.shape[-1]
    short = ref.shape[-3] * lanes - values.shape[1]
    if short > 0:
        values = jnp.concatenate([values, jnp.zeros((values.shape[0], short), F32)], axis=1)
    for k in range(ref.shape[-3]):
        ref[(*first, k, rows, slice(None))] = values[:, k * lanes : (k + 1) * lanes]


def looped(first, end, batch, compute):
    def step(block, carry):
        stores = [compute(block * batch + k) for k in range(batch)]
        for store in stores:
            store()
        return carry

    lax.fori_loop(first // batch, end // batch, step, 0)


def body(
    devices,
    slots,
    edge,
    channels,
    own_ref, low_ref, high_ref, cot_ref, mask_ref, w_in_ref, w_in_t_ref, w_out_ref, w_out_t_ref,
    update_ref, grad_ref, weights_ref,
    slabs, left, right, band, gates, saved, d_projected, tri, d_left, d_right, packed, arrived, spread,
    terms, landed, slab_send, slab_recv, pack_send, pack_recv, sum_send, sum_recv,
):
    half = slots // 2
    rows = edge * channels
    wide = slots * edge
    lanes = slabs.shape[2]
    folds = lanes // edge
    steps = devices.bit_length() - 1
    offsets = [d for d in range(-half, half + 1) if d != 0]
    me = lax.axis_index("row")

    def there(d):
        return jnp.logical_and(me + d >= 0, me + d < devices)

    partners = []
    for step in range(steps):
        bit = 1 << step
        partners.append(me + bit * (1 - 2 * lax.rem(me // bit, 2)))

    def greet(target):
        pl.semaphore_signal(
            barrier, inc=1, device_id={"row": target}, device_id_type=pl.DeviceIdType.MESH
        )

    barrier = pltpu.get_barrier_semaphore()
    for d in offsets:
        pl.when(there(d))(functools.partial(greet, me + d))
    for partner in partners:
        greet(partner)
    pl.semaphore_wait(barrier, steps + sum(there(d).astype(jnp.int32) for d in offsets))

    even = lax.rem(me, 2) == 0
    odd = jnp.logical_not(even)

    def slab_copy(source, sem, target, landing):
        return pltpu.make_async_remote_copy(
            src_ref=source,
            dst_ref=slabs.at[offsets.index(landing)],
            send_sem=slab_send.at[sem],
            recv_sem=slab_recv.at[offsets.index(landing)],
            device_id={"row": me + target},
            device_id_type=pl.DeviceIdType.MESH,
        )

    sends = [
        (there(1), slab_copy(high_ref, 0, 1, -1)),
        (there(-1), slab_copy(low_ref, 1, -1, 1)),
        (jnp.logical_and(even, there(2)), slab_copy(high_ref, 2, 2, -2)),
        (jnp.logical_and(odd, there(-2)), slab_copy(low_ref, 3, -2, 2)),
    ]
    relays = [
        (
            jnp.logical_and(even, jnp.logical_and(there(-1), there(1))),
            slab_copy(slabs.at[offsets.index(-1)], 4, 1, -2),
        ),
        (jnp.logical_and(odd, there(1)), slab_copy(slabs.at[offsets.index(1)], 5, -1, 2)),
    ]

    def pack_copy(d, landing):
        return pltpu.make_async_remote_copy(
            src_ref=packed.at[offsets.index(d)],
            dst_ref=arrived.at[offsets.index(landing)],
            send_sem=pack_send.at[offsets.index(d)],
            recv_sem=pack_recv.at[offsets.index(landing)],
            device_id={"row": me + d},
            device_id_type=pl.DeviceIdType.MESH,
        )

    for needed, copy in sends:
        pl.when(needed)(copy.start)

    w_in = w_in_ref[...]
    w_in_t = w_in_t_ref[...]
    w_out = w_out_ref[...]
    w_out_t = w_out_t_ref[...]
    mask = mask_ref[...]

    def at(i):
        return pl.ds(pl.multiple_of(i * channels, channels), channels)

    def four(i):
        return pl.ds(pl.multiple_of(i * 4 * channels, channels), 4 * channels)

    def project_own(i):
        normed, _ = unit(own_ref[at(i), :].astype(F32))
        projected = dot(w_in_t, normed.astype(BF16), NN)
        parts = []
        for group in range(2):
            low = 2 * group * channels
            parts.append(jax.nn.sigmoid(projected[low : low + channels]))
            parts.append(projected[low + channels : low + 2 * channels])
        gate = jax.nn.sigmoid(projected[4 * channels :])

        def store():
            put(left, at(i), (parts[0] * parts[1]).astype(BF16).astype(F32), half)
            put(right, at(i), (parts[2] * parts[3]).astype(BF16).astype(F32), half)
            saved[four(i), :] = jnp.concatenate(parts, axis=0)
            gates[at(i), :] = gate

        return store

    looped(0, edge, 2, project_own)

    def project_slab(d, relay):
        index = offsets.index(d)
        count = (slots - abs(d)) * edge
        skipped = max(0, -d - 1) * edge
        first = max(0, d) * edge

        def absent():
            slabs[index] = jnp.zeros((rows, lanes), BF16)

        pl.when(there(d))(lambda: slab_copy(low_ref, 0, d, d).wait_recv())
        pl.when(jnp.logical_not(there(d)))(absent)
        if relay is not None:
            pl.when(relay[0])(relay[1].start)

        def placed(values):
            parts = [values[:, skipped : skipped + count]]
            if first > 0:
                parts = [jnp.zeros((channels, first), F32)] + parts
            tail = wide - first - count
            if tail > 0:
                parts = parts + [jnp.zeros((channels, tail), F32)]
            return jnp.concatenate(parts, axis=1)

        def project_far(block):
            picked = [block * 4 + k for k in range(4)]
            values = jnp.concatenate([slabs[index, at(i), :] for i in picked], axis=1)
            normed, _ = unit(values.astype(F32))
            projected = dot(w_in_t[: 4 * channels], normed.astype(BF16), NN)
            results = [gated(projected, channels, group).astype(BF16).astype(F32) for group in range(2)]

            def store():
                for result, ref in zip(results, (left, right)):
                    for k, i in enumerate(picked):
                        put(ref, at(i), placed(result[:, k * lanes : (k + 1) * lanes]), half + d)

            return store

        looped(0, edge // 4, 1, project_far)

    pl.when(even)(lambda: project_slab(1, None))
    pl.when(odd)(lambda: project_slab(-1, None))
    pl.when(even)(lambda: project_slab(-1, relays[0]))
    pl.when(odd)(lambda: project_slab(1, relays[1]))
    project_slab(-2, None)
    project_slab(2, None)

    def triangle(c):
        every = pl.ds(c, edge, stride=channels)
        block = jnp.concatenate([taken(right, every, wide, v) for v in range(slots)], axis=0).astype(BF16)
        result = dot(taken(left, every, wide, half).astype(BF16), block, NT)

        def store():
            band[c] = block
            put(tri, every, result)

        return store

    looped(0, channels, 4, triangle)

    def middle(start, carry):
        total = carry
        d_tiles = []
        for fold in range(folds):
            i = start + fold * (edge // folds)
            normed, scale = unit(taken(tri, at(i), wide))
            normed_low = normed.astype(BF16)
            mixed = dot(w_out_t, normed_low, NN)
            gate = gates[at(i), :]
            update_ref[at(i), :] = (mask * gate * mixed).astype(BF16)
            d_update = cot_ref[at(i), :].astype(F32) * mask
            d_mixed = (d_update * gate).astype(BF16)
            d_projected[i, 4 * channels :, :] = (d_update * mixed * gate * (1.0 - gate)).astype(BF16)
            total = total + dot(normed_low, d_mixed, NT)
            d_tri = unit_back(normed, scale, dot(w_out, d_mixed, NN)).astype(BF16).astype(F32)
            put(tri, at(i), d_tri)
            d_tiles.append(d_tri)
        for d in offsets:
            v = half + d
            packed[offsets.index(d), at(start), :] = jnp.concatenate(
                [tile[:, v * edge : (v + 1) * edge] for tile in d_tiles], axis=1
            ).astype(BF16)
        return total

    grad_out = lax.fori_loop(0, edge // folds, middle, jnp.zeros((channels, channels), F32))

    for d in offsets:
        pl.when(there(d))(lambda d=d: pack_copy(d, -d).start())

    def to_left(c):
        every = pl.ds(c, edge, stride=channels)
        result = dot(taken(tri, every, wide).astype(BF16), band[c], NN)
        return lambda: put(d_left, every, result)

    looped(0, channels, 4, to_left)

    def weigh(group, ref, joined_gate):
        def compute(block, carry):
            stores = []
            for i in (2 * block, 2 * block + 1):
                normed, _ = unit(own_ref[at(i), :].astype(F32))
                held = saved[four(i), :]
                gate = held[2 * group * channels : (2 * group + 1) * channels]
                value = held[(2 * group + 1) * channels : (2 * group + 2) * channels]
                to_value = taken(ref, at(i), wide) * mask * gate
                front = jnp.concatenate([to_value * value * (1.0 - gate), to_value], axis=0).astype(BF16)
                stores.append((i, front))
                if joined_gate:
                    front = jnp.concatenate([front, d_projected[i, 4 * channels :, :]], axis=0)
                carry = carry + dot(normed.astype(BF16), front, NT)
            for i, front in stores:
                d_projected[i, 2 * group * channels : (2 * group + 2) * channels, :] = front
            return carry

        width = (3 if joined_gate else 2) * channels
        return lax.fori_loop(0, edge // 2, compute, jnp.zeros((channels, width), F32))

    def summed(total, first, sem, beside):
        width = total.shape[1]
        for step, partner in enumerate(partners):
            terms[step, :, first : first + width] = total
            copy = pltpu.make_async_remote_copy(
                src_ref=terms.at[step, :, pl.ds(first, width)],
                dst_ref=landed.at[step, :, pl.ds(first, width)],
                send_sem=sum_send.at[sem + step],
                recv_sem=sum_recv.at[sem + step],
                device_id={"row": partner},
                device_id_type=pl.DeviceIdType.MESH,
            )
            copy.start()
            beside(step)
            copy.wait()
            total = total + landed[step, :, first : first + width]
        weights_ref[:, first : first + width] = total

    early = jnp.concatenate([weigh(0, d_left, True), grad_out], axis=1)

    def take_packs():
        for d in offsets:
            index = offsets.index(d)

            def absent(index=index):
                arrived[index] = jnp.zeros(arrived.shape[1:], BF16)

            pl.when(there(d))(lambda d=d: pack_copy(d, d).wait_recv())
            pl.when(jnp.logical_not(there(d)))(absent)
            spread[index] = arrived[index].astype(F32)

    def to_right(c):
        every = pl.ds(c, edge, stride=channels)
        folded = pl.ds(c, edge // folds, stride=channels)
        pieces = []
        sources = []
        for d in range(-half, half + 1):
            sources.append(taken(left, every, wide, half + d))
            if d == 0:
                pieces.append(taken(tri, every, wide)[:, half * edge : (half + 1) * edge])
            else:
                tile = spread[offsets.index(d), folded, :]
                for fold in range(folds):
                    pieces.append(tile[:, fold * edge : (fold + 1) * edge])
        d_tile = jnp.concatenate(pieces, axis=0).astype(BF16)
        source = jnp.concatenate(sources, axis=0).astype(BF16)
        result = dot(d_tile, source, TN)
        return lambda: put(d_right, every, result)

    def beside_early(step):
        if step == 0:
            take_packs()
        looped(channels // 4 * step // steps * 4, channels // 4 * (step + 1) // steps * 4, 4, to_right)

    summed(early, 0, 0, beside_early)
    late = weigh(1, d_right, False)

    def to_pair(i):
        normed, scale = unit(own_ref[at(i), :].astype(F32))
        result = unit_back(normed, scale, dot(w_in, d_projected[i], NN)).astype(BF16)

        def store():
            grad_ref[at(i), :] = result

        return store

    def beside_late(step):
        looped(edge // 2 * step // steps * 2, edge // 2 * (step + 1) // steps * 2, 2, to_pair)

    summed(late, 4 * channels, steps, beside_late)

    for needed, copy in sends + relays:
        pl.when(needed)(copy.wait_send)
    for d in offsets:
        pl.when(there(d))(lambda d=d: pack_copy(d, -d).wait_send())


def local(pair, kept, w_in, w_out, cotangent):
    slots, edge = pair.shape[1], pair.shape[2]
    channels = w_in.shape[0]
    half = slots // 2
    rows, wide = edge * channels, slots * edge
    lanes = wide - edge
    chunks = -(-wide // lanes)
    devices = lax.axis_size("row")
    steps = devices.bit_length() - 1

    def to_columns(tiles):
        return jnp.transpose(tiles, (1, 3, 0, 2)).reshape(rows, wide)

    def from_columns(columns):
        tiles = columns.reshape(edge, channels, slots, edge)
        return jnp.transpose(tiles, (2, 0, 3, 1)).reshape(pair.shape)

    tiles = pair[0].reshape(slots, edge, edge, channels)
    own = to_columns(tiles * kept[0].astype(BF16)[:, None, None, None])
    cot = to_columns(cotangent[0].reshape(tiles.shape))
    mask = jnp.repeat(kept[0].astype(F32), edge)[None, :]
    low, high = own[:, :lanes], own[:, edge:]

    whole = pl.BlockSpec(memory_space=pltpu.VMEM)
    far = 2 * half
    update, grad, weights = pl.pallas_call(
        functools.partial(body, devices, slots, edge, channels),
        out_shape=(
            jax.ShapeDtypeStruct((rows, wide), BF16),
            jax.ShapeDtypeStruct((rows, wide), BF16),
            jax.ShapeDtypeStruct((channels, 6 * channels), F32),
        ),
        in_specs=[whole] * 9,
        out_specs=(whole, whole, whole),
        scratch_shapes=[
            pltpu.VMEM((far, rows, lanes), BF16),
            pltpu.VMEM((slots, chunks, rows, lanes), F32),
            pltpu.VMEM((slots, chunks, rows, lanes), F32),
            pltpu.VMEM((channels, wide, wide), BF16),
            pltpu.VMEM((rows, wide), F32),
            pltpu.VMEM((4 * rows, wide), F32),
            pltpu.VMEM((edge, 5 * channels, wide), BF16),
            pltpu.VMEM((chunks, rows, lanes), F32),
            pltpu.VMEM((chunks, rows, lanes), F32),
            pltpu.VMEM((chunks, rows, lanes), F32),
            pltpu.VMEM((far, rows * edge // lanes, lanes), BF16),
            pltpu.VMEM((far, rows * edge // lanes, lanes), BF16),
            pltpu.VMEM((far, rows * edge // lanes, lanes), F32),
            pltpu.VMEM((steps, channels, 6 * channels), F32),
            pltpu.VMEM((steps, channels, 6 * channels), F32),
            pltpu.SemaphoreType.DMA((far + 2,)),
            pltpu.SemaphoreType.DMA((far,)),
            pltpu.SemaphoreType.DMA((far,)),
            pltpu.SemaphoreType.DMA((far,)),
            pltpu.SemaphoreType.DMA((2 * steps,)),
            pltpu.SemaphoreType.DMA((2 * steps,)),
        ],
        compiler_params=pltpu.CompilerParams(
            collective_id=0, has_side_effects=True, vmem_limit_bytes=63 * 1024 * 1024
        ),
    )(own, low, high, cot, mask, w_in, w_in.T, w_out, w_out.T)
    first, gate, out, second = jnp.split(
        weights, [2 * channels, 3 * channels, 4 * channels], axis=1
    )
    grad_w_in = jnp.concatenate([first, second, gate], axis=1)
    grad_w_out = out
    return (from_columns(update), from_columns(grad), grad_w_in, grad_w_out)


def solution(mesh):
    tiled = P(("grp", "row"), None, None, None)
    return jax.shard_map(
        local,
        mesh=mesh,
        in_specs=(tiled, P(("grp", "row"), None), P(), P(), tiled),
        out_specs=(tiled, tiled, P("grp", None), P("grp", None)),
        check_vma=False,
    )
```

```python
import functools

import jax
import jax.numpy as jnp
from jax import lax
from jax.experimental import pallas as pl
from jax.experimental.pallas import tpu as pltpu
from jax.sharding import PartitionSpec as P

EPS = 1e-05
F32 = jnp.float32
BF16 = jnp.bfloat16
NN = (((1,), (0,)), ((), ()))
NT = (((1,), (1,)), ((), ()))
TN = (((0,), (0,)), ((), ()))


def dot(a, b, dims):
    return lax.dot_general(a, b, dims, preferred_element_type=F32)


def unit(values):
    average = jnp.mean(values, axis=0, keepdims=True)
    centered = values - average
    variance = jnp.mean(centered * centered, axis=0, keepdims=True)
    scale = lax.rsqrt(variance + EPS)
    return centered * scale, scale


def unit_back(normed, scale, incoming):
    return scale * (
        incoming
        - jnp.mean(incoming, axis=0, keepdims=True)
        - normed * jnp.mean(incoming * normed, axis=0, keepdims=True)
    )


def gated(projected, channels, group):
    gate = jax.nn.sigmoid(projected[2 * group * channels : (2 * group + 1) * channels])
    return gate * projected[(2 * group + 1) * channels : (2 * group + 2) * channels]


def taken(ref, rows, wide, *first):
    lanes = ref.shape[-1]
    chunks = [ref[(*first, k, rows, slice(None))] for k in range(ref.shape[-3])]
    return jnp.concatenate(chunks, axis=1)[:, :wide] if len(chunks) * lanes > wide else chunks[0]


def put(ref, rows, values, *first):
    lanes = ref.shape[-1]
    short = ref.shape[-3] * lanes - values.shape[1]
    if short > 0:
        values = jnp.concatenate([values, jnp.zeros((values.shape[0], short), F32)], axis=1)
    for k in range(ref.shape[-3]):
        ref[(*first, k, rows, slice(None))] = values[:, k * lanes : (k + 1) * lanes]


def looped(first, end, batch, compute):
    def step(block, carry):
        stores = [compute(block * batch + k) for k in range(batch)]
        for store in stores:
            store()
        return carry

    lax.fori_loop(first // batch, end // batch, step, 0)


def body(
    devices,
    slots,
    edge,
    channels,
    own_ref, low_ref, high_ref, cot_ref, mask_ref, w_in_ref, w_in_t_ref, w_out_ref, w_out_t_ref,
    update_ref, grad_ref, weights_ref,
    slabs, left, right, band, gates, saved, d_projected, tri, d_left, d_right, packed, arrived, spread,
    terms, landed, slab_send, slab_recv, pack_send, pack_recv, sum_send, sum_recv,
):
    half = slots // 2
    rows = edge * channels
    wide = slots * edge
    lanes = slabs.shape[2]
    folds = lanes // edge
    steps = devices.bit_length() - 1
    offsets = [d for d in range(-half, half + 1) if d != 0]
    me = lax.axis_index("row")

    def there(d):
        return jnp.logical_and(me + d >= 0, me + d < devices)

    partners = []
    for step in range(steps):
        bit = 1 << step
        partners.append(me + bit * (1 - 2 * lax.rem(me // bit, 2)))

    def greet(target):
        pl.semaphore_signal(
            barrier, inc=1, device_id={"row": target}, device_id_type=pl.DeviceIdType.MESH
        )

    barrier = pltpu.get_barrier_semaphore()
    for d in offsets:
        pl.when(there(d))(functools.partial(greet, me + d))
    for partner in partners:
        greet(partner)
    pl.semaphore_wait(barrier, steps + sum(there(d).astype(jnp.int32) for d in offsets))

    even = lax.rem(me, 2) == 0
    odd = jnp.logical_not(even)

    def slab_copy(source, sem, target, landing):
        return pltpu.make_async_remote_copy(
            src_ref=source,
            dst_ref=slabs.at[offsets.index(landing)],
            send_sem=slab_send.at[sem],
            recv_sem=slab_recv.at[offsets.index(landing)],
            device_id={"row": me + target},
            device_id_type=pl.DeviceIdType.MESH,
        )

    sends = [
        (there(1), slab_copy(high_ref, 0, 1, -1)),
        (there(-1), slab_copy(low_ref, 1, -1, 1)),
        (jnp.logical_and(even, there(2)), slab_copy(high_ref, 2, 2, -2)),
        (jnp.logical_and(odd, there(-2)), slab_copy(low_ref, 3, -2, 2)),
    ]
    relays = [
        (
            jnp.logical_and(even, jnp.logical_and(there(-1), there(1))),
            slab_copy(slabs.at[offsets.index(-1)], 4, 1, -2),
        ),
        (jnp.logical_and(odd, there(1)), slab_copy(slabs.at[offsets.index(1)], 5, -1, 2)),
    ]

    def pack_copy(d, landing):
        return pltpu.make_async_remote_copy(
            src_ref=packed.at[offsets.index(d)],
            dst_ref=arrived.at[offsets.index(landing)],
            send_sem=pack_send.at[offsets.index(d)],
            recv_sem=pack_recv.at[offsets.index(landing)],
            device_id={"row": me + d},
            device_id_type=pl.DeviceIdType.MESH,
        )

    for needed, copy in sends:
        pl.when(needed)(copy.start)

    w_in = w_in_ref[...]
    w_in_t = w_in_t_ref[...]
    w_out = w_out_ref[...]
    w_out_t = w_out_t_ref[...]
    mask = mask_ref[...]

    def at(i):
        return pl.ds(pl.multiple_of(i * channels, channels), channels)

    def four(i):
        return pl.ds(pl.multiple_of(i * 4 * channels, channels), 4 * channels)

    def project_own(i):
        normed, _ = unit(own_ref[at(i), :].astype(F32))
        projected = dot(w_in_t, normed.astype(BF16), NN)
        parts = []
        for group in range(2):
            low = 2 * group * channels
            parts.append(jax.nn.sigmoid(projected[low : low + channels]))
            parts.append(projected[low + channels : low + 2 * channels])
        gate = jax.nn.sigmoid(projected[4 * channels :])

        def store():
            put(left, at(i), (parts[0] * parts[1]).astype(BF16).astype(F32), half)
            put(right, at(i), (parts[2] * parts[3]).astype(BF16).astype(F32), half)
            saved[four(i), :] = jnp.concatenate(parts, axis=0)
            put(gates, at(i), gate)

        return store

    looped(0, edge, 2, project_own)

    def project_slab(d, relay):
        index = offsets.index(d)
        count = (slots - abs(d)) * edge
        skipped = max(0, -d - 1) * edge
        first = max(0, d) * edge

        def absent():
            slabs[index] = jnp.zeros((rows, lanes), BF16)

        pl.when(there(d))(lambda: slab_copy(low_ref, 0, d, d).wait_recv())
        pl.when(jnp.logical_not(there(d)))(absent)
        if relay is not None:
            pl.when(relay[0])(relay[1].start)

        def placed(values):
            parts = [values[:, skipped : skipped + count]]
            if first > 0:
                parts = [jnp.zeros((channels, first), F32)] + parts
            tail = wide - first - count
            if tail > 0:
                parts = parts + [jnp.zeros((channels, tail), F32)]
            return jnp.concatenate(parts, axis=1)

        def project_far(block):
            picked = [block * 4 + k for k in range(4)]
            values = jnp.concatenate([slabs[index, at(i), :] for i in picked], axis=1)
            normed, _ = unit(values.astype(F32))
            projected = dot(w_in_t[: 4 * channels], normed.astype(BF16), NN)
            results = [gated(projected, channels, group).astype(BF16).astype(F32) for group in range(2)]

            def store():
                for result, ref in zip(results, (left, right)):
                    for k, i in enumerate(picked):
                        put(ref, at(i), placed(result[:, k * lanes : (k + 1) * lanes]), half + d)

            return store

        looped(0, edge // 4, 1, project_far)

    pl.when(even)(lambda: project_slab(1, None))
    pl.when(odd)(lambda: project_slab(-1, None))

    def piece(block):
        return pl.ds(pl.multiple_of(block * 128, 128), 128)

    def cot_to_rows(block):
        values = cot_ref[:, piece(block)].astype(F32).T
        return lambda: put(d_left, piece(block), values)

    def cot_to_blocks(c):
        every = pl.ds(c, edge, stride=channels)
        turned = taken(d_left, every, wide).T
        values = jnp.concatenate([turned[w * edge : (w + 1) * edge] for w in range(slots)], axis=1)
        return lambda: put(d_right, every, values)

    looped(0, rows // 128, 2, cot_to_rows)
    looped(0, channels, 4, cot_to_blocks)
    pl.when(even)(lambda: project_slab(-1, relays[0]))
    pl.when(odd)(lambda: project_slab(1, relays[1]))
    project_slab(-2, None)
    project_slab(2, None)

    def triangle(c):
        every = pl.ds(c, edge, stride=channels)
        block = jnp.concatenate([taken(right, every, wide, v) for v in range(slots)], axis=0).astype(BF16)
        result = dot(taken(left, every, wide, half).astype(BF16), block, NT)

        def store():
            band[c] = block
            put(tri, every, result)

        return store

    looped(0, channels, 4, triangle)

    def middle(start, carry):
        total = carry
        d_tiles = []
        for fold in range(folds):
            i = start + fold * (edge // folds)
            normed, scale = unit(taken(tri, at(i), wide))
            normed_low = normed.astype(BF16)
            mixed = dot(w_out_t, normed_low, NN)
            gate = taken(gates, at(i), wide)
            put(gates, at(i), mask * gate * mixed)
            d_update = taken(d_right, at(i), wide) * mask
            d_mixed = (d_update * gate).astype(BF16)
            d_projected[i, 4 * channels :, :] = (d_update * mixed * gate * (1.0 - gate)).astype(BF16)
            total = total + dot(normed_low, d_mixed, NT)
            d_tri = unit_back(normed, scale, dot(w_out, d_mixed, NN)).astype(BF16).astype(F32)
            put(tri, at(i), d_tri)
            d_tiles.append(d_tri)
        for d in offsets:
            v = half + d
            packed[offsets.index(d), at(start), :] = jnp.concatenate(
                [tile[:, v * edge : (v + 1) * edge] for tile in d_tiles], axis=1
            ).astype(BF16)
        return total

    grad_out = lax.fori_loop(0, edge // folds, middle, jnp.zeros((channels, channels), F32))

    for d in offsets:
        pl.when(there(d))(lambda d=d: pack_copy(d, -d).start())

    def to_left(c):
        every = pl.ds(c, edge, stride=channels)
        result = dot(taken(tri, every, wide).astype(BF16), band[c], NN)
        return lambda: put(d_left, every, result)

    looped(0, channels, 4, to_left)

    def weigh(group, ref, joined_gate):
        def compute(block, carry):
            stores = []
            for i in (2 * block, 2 * block + 1):
                normed, _ = unit(own_ref[at(i), :].astype(F32))
                held = saved[four(i), :]
                gate = held[2 * group * channels : (2 * group + 1) * channels]
                value = held[(2 * group + 1) * channels : (2 * group + 2) * channels]
                to_value = taken(ref, at(i), wide) * mask * gate
                front = jnp.concatenate([to_value * value * (1.0 - gate), to_value], axis=0).astype(BF16)
                stores.append((i, front))
                if joined_gate:
                    front = jnp.concatenate([front, d_projected[i, 4 * channels :, :]], axis=0)
                carry = carry + dot(normed.astype(BF16), front, NT)
            for i, front in stores:
                d_projected[i, 2 * group * channels : (2 * group + 2) * channels, :] = front
            return carry

        width = (3 if joined_gate else 2) * channels
        return lax.fori_loop(0, edge // 2, compute, jnp.zeros((channels, width), F32))

    def summed(total, first, sem, beside):
        width = total.shape[1]
        for step, partner in enumerate(partners):
            terms[step, :, first : first + width] = total
            copy = pltpu.make_async_remote_copy(
                src_ref=terms.at[step, :, pl.ds(first, width)],
                dst_ref=landed.at[step, :, pl.ds(first, width)],
                send_sem=sum_send.at[sem + step],
                recv_sem=sum_recv.at[sem + step],
                device_id={"row": partner},
                device_id_type=pl.DeviceIdType.MESH,
            )
            copy.start()
            beside(step)
            copy.wait()
            total = total + landed[step, :, first : first + width]
        weights_ref[:, first : first + width] = total

    early = jnp.concatenate([weigh(0, d_left, True), grad_out], axis=1)

    def take_packs():
        for d in offsets:
            index = offsets.index(d)

            def absent(index=index):
                arrived[index] = jnp.zeros(arrived.shape[1:], BF16)

            pl.when(there(d))(lambda d=d: pack_copy(d, d).wait_recv())
            pl.when(jnp.logical_not(there(d)))(absent)
            spread[index] = arrived[index].astype(F32)

    def to_right(c):
        every = pl.ds(c, edge, stride=channels)
        folded = pl.ds(c, edge // folds, stride=channels)
        pieces = []
        sources = []
        for d in range(-half, half + 1):
            sources.append(taken(left, every, wide, half + d))
            if d == 0:
                pieces.append(taken(tri, every, wide)[:, half * edge : (half + 1) * edge])
            else:
                tile = spread[offsets.index(d), folded, :]
                for fold in range(folds):
                    pieces.append(tile[:, fold * edge : (fold + 1) * edge])
        d_tile = jnp.concatenate(pieces, axis=0).astype(BF16)
        source = jnp.concatenate(sources, axis=0).astype(BF16)
        result = dot(d_tile, source, TN)
        return lambda: put(d_right, every, result)

    def beside_early(step):
        if step == 0:
            take_packs()
        looped(channels // 4 * step // steps * 4, channels // 4 * (step + 1) // steps * 4, 4, to_right)

    summed(early, 0, 0, beside_early)
    late = weigh(1, d_right, False)

    def to_pair(i):
        normed, scale = unit(own_ref[at(i), :].astype(F32))
        result = unit_back(normed, scale, dot(w_in, d_projected[i], NN)).astype(BF16)

        def store():
            grad_ref[at(i), :] = result

        return store

    def update_to_rows(c):
        every = pl.ds(c, edge, stride=channels)
        values = taken(gates, every, wide)
        values = jnp.concatenate([values[:, w * edge : (w + 1) * edge] for w in range(slots)], axis=0).T
        return lambda: put(tri, every, values)

    def update_to_tiles(block):
        values = taken(tri, piece(block), wide).T.astype(BF16)

        def store():
            update_ref[:, piece(block)] = values

        return store

    def beside_late(step):
        middle_step = steps // 2
        if step < middle_step:
            blocks = channels // 4
            looped(blocks * step // middle_step * 4, blocks * (step + 1) // middle_step * 4, 4, update_to_rows)
        else:
            blocks, step_now, step_count = rows // 256, step - middle_step, steps - middle_step
            looped(blocks * step_now // step_count * 2, blocks * (step_now + 1) // step_count * 2, 2, update_to_tiles)
        looped(edge // 2 * step // steps * 2, edge // 2 * (step + 1) // steps * 2, 2, to_pair)

    summed(late, 4 * channels, steps, beside_late)

    for needed, copy in sends + relays:
        pl.when(needed)(copy.wait_send)
    for d in offsets:
        pl.when(there(d))(lambda d=d: pack_copy(d, -d).wait_send())


def local(pair, kept, w_in, w_out, cotangent):
    slots, edge = pair.shape[1], pair.shape[2]
    channels = w_in.shape[0]
    half = slots // 2
    rows, wide = edge * channels, slots * edge
    lanes = wide - edge
    chunks = -(-wide // lanes)
    devices = lax.axis_size("row")
    steps = devices.bit_length() - 1

    def to_columns(tiles):
        return jnp.transpose(tiles, (1, 3, 0, 2)).reshape(rows, wide)

    def from_columns(columns):
        tiles = columns.reshape(edge, channels, slots, edge)
        return jnp.transpose(tiles, (2, 0, 3, 1)).reshape(pair.shape)

    tiles = pair[0].reshape(slots, edge, edge, channels)
    own = to_columns(tiles * kept[0].astype(BF16)[:, None, None, None])
    cot = cotangent[0].reshape(wide, rows)
    mask = jnp.repeat(kept[0].astype(F32), edge)[None, :]
    low, high = own[:, :lanes], own[:, edge:]

    whole = pl.BlockSpec(memory_space=pltpu.VMEM)
    far = 2 * half
    update, grad, weights = pl.pallas_call(
        functools.partial(body, devices, slots, edge, channels),
        out_shape=(
            jax.ShapeDtypeStruct((wide, rows), BF16),
            jax.ShapeDtypeStruct((rows, wide), BF16),
            jax.ShapeDtypeStruct((channels, 6 * channels), F32),
        ),
        in_specs=[whole] * 9,
        out_specs=(whole, whole, whole),
        scratch_shapes=[
            pltpu.VMEM((far, rows, lanes), BF16),
            pltpu.VMEM((slots, chunks, rows, lanes), F32),
            pltpu.VMEM((slots, chunks, rows, lanes), F32),
            pltpu.VMEM((channels, wide, wide), BF16),
            pltpu.VMEM((chunks, rows, lanes), F32),
            pltpu.VMEM((4 * rows, wide), F32),
            pltpu.VMEM((edge, 5 * channels, wide), BF16),
            pltpu.VMEM((chunks, rows, lanes), F32),
            pltpu.VMEM((chunks, rows, lanes), F32),
            pltpu.VMEM((chunks, rows, lanes), F32),
            pltpu.VMEM((far, rows * edge // lanes, lanes), BF16),
            pltpu.VMEM((far, rows * edge // lanes, lanes), BF16),
            pltpu.VMEM((far, rows * edge // lanes, lanes), F32),
            pltpu.VMEM((steps, channels, 6 * channels), F32),
            pltpu.VMEM((steps, channels, 6 * channels), F32),
            pltpu.SemaphoreType.DMA((far + 2,)),
            pltpu.SemaphoreType.DMA((far,)),
            pltpu.SemaphoreType.DMA((far,)),
            pltpu.SemaphoreType.DMA((far,)),
            pltpu.SemaphoreType.DMA((2 * steps,)),
            pltpu.SemaphoreType.DMA((2 * steps,)),
        ],
        compiler_params=pltpu.CompilerParams(
            collective_id=0, has_side_effects=True, vmem_limit_bytes=63 * 1024 * 1024
        ),
    )(own, low, high, cot, mask, w_in, w_in.T, w_out, w_out.T)
    first, gate, out, second = jnp.split(
        weights, [2 * channels, 3 * channels, 4 * channels], axis=1
    )
    grad_w_in = jnp.concatenate([first, second, gate], axis=1)
    grad_w_out = out
    return (update.reshape(pair.shape), from_columns(grad), grad_w_in, grad_w_out)


def solution(mesh):
    tiled = P(("grp", "row"), None, None, None)
    return jax.shard_map(
        local,
        mesh=mesh,
        in_specs=(tiled, P(("grp", "row"), None), P(), P(), tiled),
        out_specs=(tiled, tiled, P("grp", None), P("grp", None)),
        check_vma=False,
    )
```

```python
import functools

import jax
import jax.numpy as jnp
from jax import lax
from jax.experimental import pallas as pl
from jax.experimental.pallas import tpu as pltpu
from jax.sharding import PartitionSpec as P

EPS = 1e-05
F32 = jnp.float32
BF16 = jnp.bfloat16
NN = (((1,), (0,)), ((), ()))
NT = (((1,), (1,)), ((), ()))
TN = (((0,), (0,)), ((), ()))


def dot(a, b, dims):
    return lax.dot_general(a, b, dims, preferred_element_type=F32)


def unit(values):
    average = jnp.mean(values, axis=0, keepdims=True)
    centered = values - average
    variance = jnp.mean(centered * centered, axis=0, keepdims=True)
    scale = lax.rsqrt(variance + EPS)
    return centered * scale, scale


def unit_back(normed, scale, incoming):
    return scale * (
        incoming
        - jnp.mean(incoming, axis=0, keepdims=True)
        - normed * jnp.mean(incoming * normed, axis=0, keepdims=True)
    )


def gated(projected, channels, group):
    gate = jax.nn.sigmoid(projected[2 * group * channels : (2 * group + 1) * channels])
    return gate * projected[(2 * group + 1) * channels : (2 * group + 2) * channels]


def taken(ref, rows, wide, *first):
    lanes = ref.shape[-1]
    chunks = [ref[(*first, k, rows, slice(None))] for k in range(ref.shape[-3])]
    return jnp.concatenate(chunks, axis=1)[:, :wide] if len(chunks) * lanes > wide else chunks[0]


def put(ref, rows, values, *first):
    lanes = ref.shape[-1]
    short = ref.shape[-3] * lanes - values.shape[1]
    if short > 0:
        values = jnp.concatenate([values, jnp.zeros((values.shape[0], short), F32)], axis=1)
    for k in range(ref.shape[-3]):
        ref[(*first, k, rows, slice(None))] = values[:, k * lanes : (k + 1) * lanes]


def looped(first, end, batch, compute):
    def step(block, carry):
        stores = [compute(block * batch + k) for k in range(batch)]
        for store in stores:
            store()
        return carry

    lax.fori_loop(first // batch, end // batch, step, 0)


def body(
    devices,
    slots,
    edge,
    channels,
    own_ref, low_ref, high_ref, cot_ref, mask_ref, w_in_ref, w_in_t_ref, w_out_ref, w_out_t_ref,
    update_ref, grad_ref, weights_ref,
    slabs, left, right, band, gates, saved, d_projected, tri, d_left, d_right, packed, arrived, spread,
    terms, landed, slab_send, slab_recv, pack_send, pack_recv, sum_send, sum_recv,
):
    half = slots // 2
    rows = edge * channels
    wide = slots * edge
    lanes = slabs.shape[2]
    folds = lanes // edge
    steps = devices.bit_length() - 1
    offsets = [d for d in range(-half, half + 1) if d != 0]
    me = lax.axis_index("row")

    def there(d):
        return jnp.logical_and(me + d >= 0, me + d < devices)

    partners = []
    for step in range(steps):
        bit = 1 << step
        partners.append(me + bit * (1 - 2 * lax.rem(me // bit, 2)))

    def greet(target):
        pl.semaphore_signal(
            barrier, inc=1, device_id={"row": target}, device_id_type=pl.DeviceIdType.MESH
        )

    barrier = pltpu.get_barrier_semaphore()
    for d in offsets:
        pl.when(there(d))(functools.partial(greet, me + d))
    for partner in partners:
        greet(partner)
    pl.semaphore_wait(barrier, steps + sum(there(d).astype(jnp.int32) for d in offsets))

    even = lax.rem(me, 2) == 0
    odd = jnp.logical_not(even)

    parts = 4
    size = rows // parts

    def part_of(p):
        return pl.ds(pl.multiple_of(p * size, size), size)

    def slab_copy(p, source, sem, target, landing):
        return pltpu.make_async_remote_copy(
            src_ref=source.at[part_of(p)],
            dst_ref=slabs.at[offsets.index(landing), part_of(p)],
            send_sem=slab_send.at[sem * parts + p],
            recv_sem=slab_recv.at[offsets.index(landing) * parts + p],
            device_id={"row": me + target},
            device_id_type=pl.DeviceIdType.MESH,
        )

    sends = [
        (there(1), (high_ref, 0, 1, -1)),
        (there(-1), (low_ref, 1, -1, 1)),
        (jnp.logical_and(even, there(2)), (high_ref, 2, 2, -2)),
        (jnp.logical_and(odd, there(-2)), (low_ref, 3, -2, 2)),
    ]
    relays = [
        (
            jnp.logical_and(even, jnp.logical_and(there(-1), there(1))),
            (slabs.at[offsets.index(-1)], 4, 1, -2),
        ),
        (jnp.logical_and(odd, there(1)), (slabs.at[offsets.index(1)], 5, -1, 2)),
    ]

    def pack_copy(d, landing):
        return pltpu.make_async_remote_copy(
            src_ref=packed.at[offsets.index(d)],
            dst_ref=arrived.at[offsets.index(landing)],
            send_sem=pack_send.at[offsets.index(d)],
            recv_sem=pack_recv.at[offsets.index(landing)],
            device_id={"row": me + d},
            device_id_type=pl.DeviceIdType.MESH,
        )

    for p in range(parts):
        for needed, route in sends:
            pl.when(needed)(lambda p=p, route=route: slab_copy(p, *route).start())

    w_in = w_in_ref[...]
    w_in_t = w_in_t_ref[...]
    w_out = w_out_ref[...]
    w_out_t = w_out_t_ref[...]
    mask = mask_ref[...]

    def at(i):
        return pl.ds(pl.multiple_of(i * channels, channels), channels)

    def four(i):
        return pl.ds(pl.multiple_of(i * 4 * channels, channels), 4 * channels)

    def project_own(i):
        normed, _ = unit(own_ref[at(i), :].astype(F32))
        projected = dot(w_in_t, normed.astype(BF16), NN)
        parts = []
        for group in range(2):
            low = 2 * group * channels
            parts.append(jax.nn.sigmoid(projected[low : low + channels]))
            parts.append(projected[low + channels : low + 2 * channels])
        gate = jax.nn.sigmoid(projected[4 * channels :])

        def store():
            put(left, at(i), (parts[0] * parts[1]).astype(BF16).astype(F32), half)
            put(right, at(i), (parts[2] * parts[3]).astype(BF16).astype(F32), half)
            saved[four(i), :] = jnp.concatenate(parts, axis=0)
            put(gates, at(i), gate)

        return store

    looped(0, edge, 2, project_own)

    def project_slab(p, d, relay):
        index = offsets.index(d)
        count = (slots - abs(d)) * edge
        skipped = max(0, -d - 1) * edge
        first = max(0, d) * edge

        def absent():
            slabs[index, part_of(p), :] = jnp.zeros((size, lanes), BF16)

        pl.when(there(d))(lambda: slab_copy(p, low_ref, 0, d, d).wait_recv())
        pl.when(jnp.logical_not(there(d)))(absent)
        if relay is not None:
            pl.when(relay[0])(lambda: slab_copy(p, *relay[1]).start())

        def placed(values):
            parts = [values[:, skipped : skipped + count]]
            if first > 0:
                parts = [jnp.zeros((channels, first), F32)] + parts
            tail = wide - first - count
            if tail > 0:
                parts = parts + [jnp.zeros((channels, tail), F32)]
            return jnp.concatenate(parts, axis=1)

        def project_far(block):
            picked = [block * 4 + k for k in range(4)]
            values = jnp.concatenate([slabs[index, at(i), :] for i in picked], axis=1)
            normed, _ = unit(values.astype(F32))
            projected = dot(w_in_t[: 4 * channels], normed.astype(BF16), NN)
            results = [gated(projected, channels, group).astype(BF16).astype(F32) for group in range(2)]

            def store():
                for result, ref in zip(results, (left, right)):
                    for k, i in enumerate(picked):
                        put(ref, at(i), placed(result[:, k * lanes : (k + 1) * lanes]), half + d)

            return store

        blocks = edge // 4 // parts
        looped(p * blocks, (p + 1) * blocks, 1, project_far)

    def same_chip(p, carry):
        pl.when(even)(lambda: project_slab(p, 1, None))
        pl.when(odd)(lambda: project_slab(p, -1, None))
        return carry

    lax.fori_loop(0, parts, same_chip, 0)

    def piece(block):
        return pl.ds(pl.multiple_of(block * 128, 128), 128)

    def cot_to_rows(block):
        values = cot_ref[:, piece(block)].astype(F32).T
        return lambda: put(d_left, piece(block), values)

    def cot_to_blocks(c):
        every = pl.ds(c, edge, stride=channels)
        turned = taken(d_left, every, wide).T
        values = jnp.concatenate([turned[w * edge : (w + 1) * edge] for w in range(slots)], axis=1)
        return lambda: put(d_right, every, values)

    looped(0, rows // 128, 2, cot_to_rows)
    looped(0, channels, 4, cot_to_blocks)
    def other_chip(p, carry):
        pl.when(even)(lambda: project_slab(p, -1, relays[0]))
        pl.when(odd)(lambda: project_slab(p, 1, relays[1]))
        project_slab(p, -2, None)
        project_slab(p, 2, None)
        return carry

    lax.fori_loop(0, parts, other_chip, 0)

    def triangle(c):
        every = pl.ds(c, edge, stride=channels)
        block = jnp.concatenate([taken(right, every, wide, v) for v in range(slots)], axis=0).astype(BF16)
        result = dot(taken(left, every, wide, half).astype(BF16), block, NT)

        def store():
            band[c] = block
            put(tri, every, result)

        return store

    looped(0, channels, 4, triangle)

    def middle(start, carry):
        total = carry
        d_tiles = []
        for fold in range(folds):
            i = start + fold * (edge // folds)
            normed, scale = unit(taken(tri, at(i), wide))
            normed_low = normed.astype(BF16)
            mixed = dot(w_out_t, normed_low, NN)
            gate = taken(gates, at(i), wide)
            put(gates, at(i), mask * gate * mixed)
            d_update = taken(d_right, at(i), wide) * mask
            d_mixed = (d_update * gate).astype(BF16)
            d_projected[i, 4 * channels :, :] = (d_update * mixed * gate * (1.0 - gate)).astype(BF16)
            total = total + dot(normed_low, d_mixed, NT)
            d_tri = unit_back(normed, scale, dot(w_out, d_mixed, NN)).astype(BF16).astype(F32)
            put(tri, at(i), d_tri)
            d_tiles.append(d_tri)
        for d in offsets:
            v = half + d
            packed[offsets.index(d), at(start), :] = jnp.concatenate(
                [tile[:, v * edge : (v + 1) * edge] for tile in d_tiles], axis=1
            ).astype(BF16)
        return total

    grad_out = lax.fori_loop(0, edge // folds, middle, jnp.zeros((channels, channels), F32))

    for d in offsets:
        pl.when(there(d))(lambda d=d: pack_copy(d, -d).start())

    def to_left(c):
        every = pl.ds(c, edge, stride=channels)
        result = dot(taken(tri, every, wide).astype(BF16), band[c], NN)
        return lambda: put(d_left, every, result)

    looped(0, channels, 4, to_left)

    def weigh(group, ref, joined_gate):
        def compute(block, carry):
            stores = []
            for i in (2 * block, 2 * block + 1):
                normed, _ = unit(own_ref[at(i), :].astype(F32))
                held = saved[four(i), :]
                gate = held[2 * group * channels : (2 * group + 1) * channels]
                value = held[(2 * group + 1) * channels : (2 * group + 2) * channels]
                to_value = taken(ref, at(i), wide) * mask * gate
                front = jnp.concatenate([to_value * value * (1.0 - gate), to_value], axis=0).astype(BF16)
                stores.append((i, front))
                if joined_gate:
                    front = jnp.concatenate([front, d_projected[i, 4 * channels :, :]], axis=0)
                carry = carry + dot(normed.astype(BF16), front, NT)
            for i, front in stores:
                d_projected[i, 2 * group * channels : (2 * group + 2) * channels, :] = front
            return carry

        width = (3 if joined_gate else 2) * channels
        return lax.fori_loop(0, edge // 2, compute, jnp.zeros((channels, width), F32))

    def summed(total, first, sem, beside):
        width = total.shape[1]
        for step, partner in enumerate(partners):
            terms[step, :, first : first + width] = total
            copy = pltpu.make_async_remote_copy(
                src_ref=terms.at[step, :, pl.ds(first, width)],
                dst_ref=landed.at[step, :, pl.ds(first, width)],
                send_sem=sum_send.at[sem + step],
                recv_sem=sum_recv.at[sem + step],
                device_id={"row": partner},
                device_id_type=pl.DeviceIdType.MESH,
            )
            copy.start()
            beside(step)
            copy.wait()
            total = total + landed[step, :, first : first + width]
        weights_ref[:, first : first + width] = total

    early = jnp.concatenate([weigh(0, d_left, True), grad_out], axis=1)

    def take_packs():
        for d in offsets:
            index = offsets.index(d)

            def absent(index=index):
                arrived[index] = jnp.zeros(arrived.shape[1:], BF16)

            pl.when(there(d))(lambda d=d: pack_copy(d, d).wait_recv())
            pl.when(jnp.logical_not(there(d)))(absent)
            spread[index] = arrived[index].astype(F32)

    def to_right(c):
        every = pl.ds(c, edge, stride=channels)
        folded = pl.ds(c, edge // folds, stride=channels)
        pieces = []
        sources = []
        for d in range(-half, half + 1):
            sources.append(taken(left, every, wide, half + d))
            if d == 0:
                pieces.append(taken(tri, every, wide)[:, half * edge : (half + 1) * edge])
            else:
                tile = spread[offsets.index(d), folded, :]
                for fold in range(folds):
                    pieces.append(tile[:, fold * edge : (fold + 1) * edge])
        d_tile = jnp.concatenate(pieces, axis=0).astype(BF16)
        source = jnp.concatenate(sources, axis=0).astype(BF16)
        result = dot(d_tile, source, TN)
        return lambda: put(d_right, every, result)

    def beside_early(step):
        if step == 0:
            take_packs()
        looped(channels // 4 * step // steps * 4, channels // 4 * (step + 1) // steps * 4, 4, to_right)

    summed(early, 0, 0, beside_early)
    late = weigh(1, d_right, False)

    def to_pair(i):
        normed, scale = unit(own_ref[at(i), :].astype(F32))
        result = unit_back(normed, scale, dot(w_in, d_projected[i], NN)).astype(BF16)

        def store():
            grad_ref[at(i), :] = result

        return store

    def update_to_rows(c):
        every = pl.ds(c, edge, stride=channels)
        values = taken(gates, every, wide)
        values = jnp.concatenate([values[:, w * edge : (w + 1) * edge] for w in range(slots)], axis=0).T
        return lambda: put(tri, every, values)

    def update_to_tiles(block):
        values = taken(tri, piece(block), wide).T.astype(BF16)

        def store():
            update_ref[:, piece(block)] = values

        return store

    def beside_late(step):
        middle_step = steps // 2
        if step < middle_step:
            blocks = channels // 4
            looped(blocks * step // middle_step * 4, blocks * (step + 1) // middle_step * 4, 4, update_to_rows)
        else:
            blocks, step_now, step_count = rows // 256, step - middle_step, steps - middle_step
            looped(blocks * step_now // step_count * 2, blocks * (step_now + 1) // step_count * 2, 2, update_to_tiles)
        looped(edge // 2 * step // steps * 2, edge // 2 * (step + 1) // steps * 2, 2, to_pair)

    summed(late, 4 * channels, steps, beside_late)

    for p in range(parts):
        for needed, route in sends + relays:
            pl.when(needed)(lambda p=p, route=route: slab_copy(p, *route).wait_send())
    for d in offsets:
        pl.when(there(d))(lambda d=d: pack_copy(d, -d).wait_send())


def local(pair, kept, w_in, w_out, cotangent):
    slots, edge = pair.shape[1], pair.shape[2]
    channels = w_in.shape[0]
    half = slots // 2
    rows, wide = edge * channels, slots * edge
    lanes = wide - edge
    chunks = -(-wide // lanes)
    devices = lax.axis_size("row")
    steps = devices.bit_length() - 1

    def to_columns(tiles):
        return jnp.transpose(tiles, (1, 3, 0, 2)).reshape(rows, wide)

    def from_columns(columns):
        tiles = columns.reshape(edge, channels, slots, edge)
        return jnp.transpose(tiles, (2, 0, 3, 1)).reshape(pair.shape)

    tiles = pair[0].reshape(slots, edge, edge, channels)
    own = to_columns(tiles * kept[0].astype(BF16)[:, None, None, None])
    cot = cotangent[0].reshape(wide, rows)
    mask = jnp.repeat(kept[0].astype(F32), edge)[None, :]
    low, high = own[:, :lanes], own[:, edge:]

    whole = pl.BlockSpec(memory_space=pltpu.VMEM)
    far = 2 * half
    update, grad, weights = pl.pallas_call(
        functools.partial(body, devices, slots, edge, channels),
        out_shape=(
            jax.ShapeDtypeStruct((wide, rows), BF16),
            jax.ShapeDtypeStruct((rows, wide), BF16),
            jax.ShapeDtypeStruct((channels, 6 * channels), F32),
        ),
        in_specs=[whole] * 9,
        out_specs=(whole, whole, whole),
        scratch_shapes=[
            pltpu.VMEM((far, rows, lanes), BF16),
            pltpu.VMEM((slots, chunks, rows, lanes), F32),
            pltpu.VMEM((slots, chunks, rows, lanes), F32),
            pltpu.VMEM((channels, wide, wide), BF16),
            pltpu.VMEM((chunks, rows, lanes), F32),
            pltpu.VMEM((4 * rows, wide), F32),
            pltpu.VMEM((edge, 5 * channels, wide), BF16),
            pltpu.VMEM((chunks, rows, lanes), F32),
            pltpu.VMEM((chunks, rows, lanes), F32),
            pltpu.VMEM((chunks, rows, lanes), F32),
            pltpu.VMEM((far, rows * edge // lanes, lanes), BF16),
            pltpu.VMEM((far, rows * edge // lanes, lanes), BF16),
            pltpu.VMEM((far, rows * edge // lanes, lanes), F32),
            pltpu.VMEM((steps, channels, 6 * channels), F32),
            pltpu.VMEM((steps, channels, 6 * channels), F32),
            pltpu.SemaphoreType.DMA((4 * (far + 2),)),
            pltpu.SemaphoreType.DMA((4 * far,)),
            pltpu.SemaphoreType.DMA((far,)),
            pltpu.SemaphoreType.DMA((far,)),
            pltpu.SemaphoreType.DMA((2 * steps,)),
            pltpu.SemaphoreType.DMA((2 * steps,)),
        ],
        compiler_params=pltpu.CompilerParams(
            collective_id=0, has_side_effects=True, vmem_limit_bytes=63 * 1024 * 1024
        ),
    )(own, low, high, cot, mask, w_in, w_in.T, w_out, w_out.T)
    first, gate, out, second = jnp.split(
        weights, [2 * channels, 3 * channels, 4 * channels], axis=1
    )
    grad_w_in = jnp.concatenate([first, second, gate], axis=1)
    grad_w_out = out
    return (update.reshape(pair.shape), from_columns(grad), grad_w_in, grad_w_out)


def solution(mesh):
    tiled = P(("grp", "row"), None, None, None)
    return jax.shard_map(
        local,
        mesh=mesh,
        in_specs=(tiled, P(("grp", "row"), None), P(), P(), tiled),
        out_specs=(tiled, tiled, P("grp", None), P("grp", None)),
        check_vma=False,
    )
```

```python
import functools

import jax
import jax.numpy as jnp
from jax import lax
from jax.experimental import pallas as pl
from jax.experimental.pallas import tpu as pltpu
from jax.sharding import PartitionSpec as P

EPS = 1e-05
F32 = jnp.float32
BF16 = jnp.bfloat16
NN = (((1,), (0,)), ((), ()))
NT = (((1,), (1,)), ((), ()))
TN = (((0,), (0,)), ((), ()))


def dot(a, b, dims):
    return lax.dot_general(a, b, dims, preferred_element_type=F32)


def unit(values):
    average = jnp.mean(values, axis=0, keepdims=True)
    centered = values - average
    variance = jnp.mean(centered * centered, axis=0, keepdims=True)
    scale = lax.rsqrt(variance + EPS)
    return centered * scale, scale


def unit_back(normed, scale, incoming):
    return scale * (
        incoming
        - jnp.mean(incoming, axis=0, keepdims=True)
        - normed * jnp.mean(incoming * normed, axis=0, keepdims=True)
    )


def gated(projected, channels, group):
    gate = jax.nn.sigmoid(projected[2 * group * channels : (2 * group + 1) * channels])
    return gate * projected[(2 * group + 1) * channels : (2 * group + 2) * channels]


def taken(ref, rows, wide, *first):
    lanes = ref.shape[-1]
    chunks = [ref[(*first, k, rows, slice(None))] for k in range(ref.shape[-3])]
    return jnp.concatenate(chunks, axis=1)[:, :wide] if len(chunks) * lanes > wide else chunks[0]


def put(ref, rows, values, *first):
    lanes = ref.shape[-1]
    short = ref.shape[-3] * lanes - values.shape[1]
    if short > 0:
        values = jnp.concatenate([values, jnp.zeros((values.shape[0], short), F32)], axis=1)
    for k in range(ref.shape[-3]):
        ref[(*first, k, rows, slice(None))] = values[:, k * lanes : (k + 1) * lanes]


def looped(first, end, batch, compute):
    def step(block, carry):
        stores = [compute(block * batch + k) for k in range(batch)]
        for store in stores:
            store()
        return carry

    lax.fori_loop(first // batch, end // batch, step, 0)


def body(
    devices,
    slots,
    edge,
    channels,
    own_ref, low_ref, high_ref, cot_ref, mask_ref, w_in_ref, w_in_t_ref, w_out_ref, w_out_t_ref,
    update_ref, grad_ref, weights_ref,
    slabs, left, right, band, gates, saved, d_projected, tri, d_left, d_right, packed, arrived, spread,
    terms, landed, slab_send, slab_recv, pack_send, pack_recv, sum_send, sum_recv,
):
    half = slots // 2
    rows = edge * channels
    wide = slots * edge
    lanes = slabs.shape[2]
    folds = lanes // edge
    steps = devices.bit_length() - 1
    offsets = [d for d in range(-half, half + 1) if d != 0]
    me = lax.axis_index("row")

    def there(d):
        return jnp.logical_and(me + d >= 0, me + d < devices)

    partners = []
    for step in range(steps):
        bit = 1 << step
        partners.append(me + bit * (1 - 2 * lax.rem(me // bit, 2)))

    def greet(target):
        pl.semaphore_signal(
            barrier, inc=1, device_id={"row": target}, device_id_type=pl.DeviceIdType.MESH
        )

    barrier = pltpu.get_barrier_semaphore()
    for d in offsets:
        pl.when(there(d))(functools.partial(greet, me + d))
    for partner in partners:
        greet(partner)
    pl.semaphore_wait(barrier, steps + sum(there(d).astype(jnp.int32) for d in offsets))

    even = lax.rem(me, 2) == 0
    odd = jnp.logical_not(even)

    parts = 4
    size = rows // parts

    def part_of(p):
        return pl.ds(pl.multiple_of(p * size, size), size)

    def slab_copy(p, source, sem, target, landing):
        return pltpu.make_async_remote_copy(
            src_ref=source.at[part_of(p)],
            dst_ref=slabs.at[offsets.index(landing), part_of(p)],
            send_sem=slab_send.at[sem * parts + p],
            recv_sem=slab_recv.at[offsets.index(landing) * parts + p],
            device_id={"row": me + target},
            device_id_type=pl.DeviceIdType.MESH,
        )

    sends = [
        (there(1), (high_ref, 0, 1, -1)),
        (there(-1), (low_ref, 1, -1, 1)),
        (jnp.logical_and(even, there(2)), (high_ref, 2, 2, -2)),
        (jnp.logical_and(odd, there(-2)), (low_ref, 3, -2, 2)),
    ]
    relays = [
        (
            jnp.logical_and(even, jnp.logical_and(there(-1), there(1))),
            (slabs.at[offsets.index(-1)], 4, 1, -2),
        ),
        (jnp.logical_and(odd, there(1)), (slabs.at[offsets.index(1)], 5, -1, 2)),
    ]

    def pack_copy(d, landing):
        return pltpu.make_async_remote_copy(
            src_ref=packed.at[offsets.index(d)],
            dst_ref=arrived.at[offsets.index(landing)],
            send_sem=pack_send.at[offsets.index(d)],
            recv_sem=pack_recv.at[offsets.index(landing)],
            device_id={"row": me + d},
            device_id_type=pl.DeviceIdType.MESH,
        )

    for p in range(parts):
        for needed, route in sends:
            pl.when(needed)(lambda p=p, route=route: slab_copy(p, *route).start())

    w_in = w_in_ref[...]
    w_in_t = w_in_t_ref[...]
    w_out = w_out_ref[...]
    w_out_t = w_out_t_ref[...]
    mask = mask_ref[...]

    def at(i):
        return pl.ds(pl.multiple_of(i * channels, channels), channels)

    def four(i):
        return pl.ds(pl.multiple_of(i * 4 * channels, channels), 4 * channels)

    def project_own(i):
        normed, _ = unit(own_ref[at(i), :].astype(F32))
        projected = dot(w_in_t, normed.astype(BF16), NN)
        parts = []
        for group in range(2):
            low = 2 * group * channels
            parts.append(jax.nn.sigmoid(projected[low : low + channels]))
            parts.append(projected[low + channels : low + 2 * channels])
        gate = jax.nn.sigmoid(projected[4 * channels :])

        def store():
            put(left, at(i), (parts[0] * parts[1]).astype(BF16).astype(F32), half)
            put(right, at(i), (parts[2] * parts[3]).astype(BF16).astype(F32), half)
            saved[four(i), :] = jnp.concatenate(parts, axis=0)
            put(gates, at(i), gate)

        return store

    looped(0, edge, 2, project_own)

    def project_slab(p, d, relay):
        index = offsets.index(d)
        count = (slots - abs(d)) * edge
        skipped = max(0, -d - 1) * edge
        first = max(0, d) * edge

        def absent():
            slabs[index, part_of(p), :] = jnp.zeros((size, lanes), BF16)

        pl.when(there(d))(lambda: slab_copy(p, low_ref, 0, d, d).wait_recv())
        pl.when(jnp.logical_not(there(d)))(absent)
        if relay is not None:
            pl.when(relay[0])(lambda: slab_copy(p, *relay[1]).start())

        def placed(values):
            parts = [values[:, skipped : skipped + count]]
            if first > 0:
                parts = [jnp.zeros((channels, first), F32)] + parts
            tail = wide - first - count
            if tail > 0:
                parts = parts + [jnp.zeros((channels, tail), F32)]
            return jnp.concatenate(parts, axis=1)

        def project_far(block):
            picked = [block * 4 + k for k in range(4)]
            values = jnp.concatenate([slabs[index, at(i), :] for i in picked], axis=1)
            normed, _ = unit(values.astype(F32))
            projected = dot(w_in_t[: 4 * channels], normed.astype(BF16), NN)
            results = [gated(projected, channels, group).astype(BF16).astype(F32) for group in range(2)]

            def store():
                for result, ref in zip(results, (left, right)):
                    for k, i in enumerate(picked):
                        put(ref, at(i), placed(result[:, k * lanes : (k + 1) * lanes]), half + d)

            return store

        blocks = edge // 4 // parts
        looped(p * blocks, (p + 1) * blocks, 1, project_far)

    def same_chip(p, carry):
        pl.when(even)(lambda: project_slab(p, 1, None))
        pl.when(odd)(lambda: project_slab(p, -1, None))
        return carry

    lax.fori_loop(0, parts, same_chip, 0)

    def piece(block):
        return pl.ds(pl.multiple_of(block * 128, 128), 128)

    def cot_to_rows(block):
        values = cot_ref[:, piece(block)].astype(F32).T
        return lambda: put(d_left, piece(block), values)

    def cot_to_blocks(c):
        every = pl.ds(c, edge, stride=channels)
        turned = taken(d_left, every, wide).T
        values = jnp.concatenate([turned[w * edge : (w + 1) * edge] for w in range(slots)], axis=1)
        return lambda: put(d_right, every, values)

    looped(0, rows // 128, 2, cot_to_rows)
    looped(0, channels, 4, cot_to_blocks)
    def other_chip(p, carry):
        pl.when(even)(lambda: project_slab(p, -1, relays[0]))
        pl.when(odd)(lambda: project_slab(p, 1, relays[1]))
        project_slab(p, -2, None)
        project_slab(p, 2, None)
        return carry

    lax.fori_loop(0, parts, other_chip, 0)

    def triangle(c):
        every = pl.ds(c, edge, stride=channels)
        block = jnp.concatenate([taken(right, every, wide, v) for v in range(slots)], axis=0).astype(BF16)
        result = dot(taken(left, every, wide, half).astype(BF16), block, NT)

        def store():
            band[c] = block
            put(tri, every, result)

        return store

    looped(0, channels, 4, triangle)

    def middle(start, carry):
        total = carry
        d_tiles = []
        for fold in range(folds):
            i = start + fold * (edge // folds)
            normed, scale = unit(taken(tri, at(i), wide))
            normed_low = normed.astype(BF16)
            mixed = dot(w_out_t, normed_low, NN)
            gate = taken(gates, at(i), wide)
            put(gates, at(i), mask * gate * mixed)
            d_update = taken(d_right, at(i), wide) * mask
            d_mixed = (d_update * gate).astype(BF16)
            d_projected[i, 4 * channels :, :] = (d_update * mixed * gate * (1.0 - gate)).astype(BF16)
            total = total + dot(normed_low, d_mixed, NT)
            d_tri = unit_back(normed, scale, dot(w_out, d_mixed, NN)).astype(BF16).astype(F32)
            put(tri, at(i), d_tri)
            d_tiles.append(d_tri)
        for d in offsets:
            v = half + d
            packed[offsets.index(d), at(start), :] = jnp.concatenate(
                [tile[:, v * edge : (v + 1) * edge] for tile in d_tiles], axis=1
            ).astype(BF16)
        return total

    grad_out = lax.fori_loop(0, edge // folds, middle, jnp.zeros((channels, channels), F32))

    for d in offsets:
        pl.when(there(d))(lambda d=d: pack_copy(d, -d).start())

    def to_left(c):
        every = pl.ds(c, edge, stride=channels)
        result = dot(taken(tri, every, wide).astype(BF16), band[c], NN)
        return lambda: put(d_left, every, result)

    looped(0, channels, 4, to_left)

    def weigh(group, ref, joined_gate):
        def compute(block, carry):
            stores = []
            for i in (2 * block, 2 * block + 1):
                normed, _ = unit(own_ref[at(i), :].astype(F32))
                held = saved[four(i), :]
                gate = held[2 * group * channels : (2 * group + 1) * channels]
                value = held[(2 * group + 1) * channels : (2 * group + 2) * channels]
                to_value = taken(ref, at(i), wide) * mask * gate
                front = jnp.concatenate([to_value * value * (1.0 - gate), to_value], axis=0).astype(BF16)
                stores.append((i, front))
                if joined_gate:
                    front = jnp.concatenate([front, d_projected[i, 4 * channels :, :]], axis=0)
                carry = carry + dot(normed.astype(BF16), front, NT)
            for i, front in stores:
                d_projected[i, 2 * group * channels : (2 * group + 2) * channels, :] = front
            return carry

        width = (3 if joined_gate else 2) * channels
        return lax.fori_loop(0, edge // 2, compute, jnp.zeros((channels, width), F32))

    def summed(total, first, sem, beside):
        width = total.shape[1]
        for step, partner in enumerate(partners):
            terms[step, :, first : first + width] = total
            copy = pltpu.make_async_remote_copy(
                src_ref=terms.at[step, :, pl.ds(first, width)],
                dst_ref=landed.at[step, :, pl.ds(first, width)],
                send_sem=sum_send.at[sem + step],
                recv_sem=sum_recv.at[sem + step],
                device_id={"row": partner},
                device_id_type=pl.DeviceIdType.MESH,
            )
            copy.start()
            beside(step)
            copy.wait()
            total = total + landed[step, :, first : first + width]
        weights_ref[:, first : first + width] = total

    early = jnp.concatenate([weigh(0, d_left, True), grad_out], axis=1)

    def take_packs():
        for d in offsets:
            index = offsets.index(d)

            def absent(index=index):
                arrived[index] = jnp.zeros(arrived.shape[1:], BF16)

            pl.when(there(d))(lambda d=d: pack_copy(d, d).wait_recv())
            pl.when(jnp.logical_not(there(d)))(absent)
            spread[index] = arrived[index].astype(F32)

    def to_right(c):
        every = pl.ds(c, edge, stride=channels)
        folded = pl.ds(c, edge // folds, stride=channels)
        pieces = []
        sources = []
        for d in range(-half, half + 1):
            sources.append(taken(left, every, wide, half + d))
            if d == 0:
                pieces.append(taken(tri, every, wide)[:, half * edge : (half + 1) * edge])
            else:
                tile = spread[offsets.index(d), folded, :]
                for fold in range(folds):
                    pieces.append(tile[:, fold * edge : (fold + 1) * edge])
        d_tile = jnp.concatenate(pieces, axis=0).astype(BF16)
        source = jnp.concatenate(sources, axis=0).astype(BF16)
        result = dot(d_tile, source, TN)
        return lambda: put(d_right, every, result)

    def beside_early(step):
        if step == 0:
            take_packs()
        looped(channels // 4 * step // steps * 4, channels // 4 * (step + 1) // steps * 4, 4, to_right)

    summed(early, 0, 0, beside_early)
    late = weigh(1, d_right, False)

    def to_pair(i):
        normed, scale = unit(own_ref[at(i), :].astype(F32))
        result = unit_back(normed, scale, dot(w_in, d_projected[i], NN))
        return lambda: put(d_left, at(i), result)

    def to_rows(source, target, c):
        every = pl.ds(c, edge, stride=channels)
        values = taken(source, every, wide)
        values = jnp.concatenate([values[:, w * edge : (w + 1) * edge] for w in range(slots)], axis=0).T
        return lambda: put(target, every, values)

    def to_tiles(source, target, block):
        values = taken(source, piece(block), wide).T.astype(BF16)

        def store():
            target[:, piece(block)] = values

        return store

    work = [
        (edge, 2, to_pair),
        (channels, 4, functools.partial(to_rows, d_left, d_right)),
        (rows // 128, 2, functools.partial(to_tiles, d_right, grad_ref)),
        (channels, 4, functools.partial(to_rows, gates, tri)),
        (rows // 128, 2, functools.partial(to_tiles, tri, update_ref)),
    ]

    def beside_late(step):
        for place, (count, batch, compute) in enumerate(work):
            if place * steps // len(work) == step:
                looped(0, count, batch, compute)

    summed(late, 4 * channels, steps, beside_late)

    for p in range(parts):
        for needed, route in sends + relays:
            pl.when(needed)(lambda p=p, route=route: slab_copy(p, *route).wait_send())
    for d in offsets:
        pl.when(there(d))(lambda d=d: pack_copy(d, -d).wait_send())


def local(pair, kept, w_in, w_out, cotangent):
    slots, edge = pair.shape[1], pair.shape[2]
    channels = w_in.shape[0]
    half = slots // 2
    rows, wide = edge * channels, slots * edge
    lanes = wide - edge
    chunks = -(-wide // lanes)
    devices = lax.axis_size("row")
    steps = devices.bit_length() - 1

    def to_columns(tiles):
        return jnp.transpose(tiles, (1, 3, 0, 2)).reshape(rows, wide)

    tiles = pair[0].reshape(slots, edge, edge, channels)
    own = to_columns(tiles * kept[0].astype(BF16)[:, None, None, None])
    cot = cotangent[0].reshape(wide, rows)
    mask = jnp.repeat(kept[0].astype(F32), edge)[None, :]
    low, high = own[:, :lanes], own[:, edge:]

    whole = pl.BlockSpec(memory_space=pltpu.VMEM)
    far = 2 * half
    update, grad, weights = pl.pallas_call(
        functools.partial(body, devices, slots, edge, channels),
        out_shape=(
            jax.ShapeDtypeStruct((wide, rows), BF16),
            jax.ShapeDtypeStruct((wide, rows), BF16),
            jax.ShapeDtypeStruct((channels, 6 * channels), F32),
        ),
        in_specs=[whole] * 9,
        out_specs=(whole, whole, whole),
        scratch_shapes=[
            pltpu.VMEM((far, rows, lanes), BF16),
            pltpu.VMEM((slots, chunks, rows, lanes), F32),
            pltpu.VMEM((slots, chunks, rows, lanes), F32),
            pltpu.VMEM((channels, wide, wide), BF16),
            pltpu.VMEM((chunks, rows, lanes), F32),
            pltpu.VMEM((4 * rows, wide), F32),
            pltpu.VMEM((edge, 5 * channels, wide), BF16),
            pltpu.VMEM((chunks, rows, lanes), F32),
            pltpu.VMEM((chunks, rows, lanes), F32),
            pltpu.VMEM((chunks, rows, lanes), F32),
            pltpu.VMEM((far, rows * edge // lanes, lanes), BF16),
            pltpu.VMEM((far, rows * edge // lanes, lanes), BF16),
            pltpu.VMEM((far, rows * edge // lanes, lanes), F32),
            pltpu.VMEM((steps, channels, 6 * channels), F32),
            pltpu.VMEM((steps, channels, 6 * channels), F32),
            pltpu.SemaphoreType.DMA((4 * (far + 2),)),
            pltpu.SemaphoreType.DMA((4 * far,)),
            pltpu.SemaphoreType.DMA((far,)),
            pltpu.SemaphoreType.DMA((far,)),
            pltpu.SemaphoreType.DMA((2 * steps,)),
            pltpu.SemaphoreType.DMA((2 * steps,)),
        ],
        compiler_params=pltpu.CompilerParams(
            collective_id=0, has_side_effects=True, vmem_limit_bytes=63 * 1024 * 1024
        ),
    )(own, low, high, cot, mask, w_in, w_in.T, w_out, w_out.T)
    first, gate, out, second = jnp.split(
        weights, [2 * channels, 3 * channels, 4 * channels], axis=1
    )
    grad_w_in = jnp.concatenate([first, second, gate], axis=1)
    grad_w_out = out
    return (update.reshape(pair.shape), grad.reshape(pair.shape), grad_w_in, grad_w_out)


def solution(mesh):
    tiled = P(("grp", "row"), None, None, None)
    return jax.shard_map(
        local,
        mesh=mesh,
        in_specs=(tiled, P(("grp", "row"), None), P(), P(), tiled),
        out_specs=(tiled, tiled, P("grp", None), P("grp", None)),
        check_vma=False,
    )
```

```python
import functools

import jax
import jax.numpy as jnp
from jax import lax
from jax.experimental import pallas as pl
from jax.experimental.pallas import tpu as pltpu
from jax.sharding import PartitionSpec as P

EPS = 1e-05
F32 = jnp.float32
BF16 = jnp.bfloat16
NN = (((1,), (0,)), ((), ()))
NT = (((1,), (1,)), ((), ()))
TN = (((0,), (0,)), ((), ()))


def dot(a, b, dims):
    return lax.dot_general(a, b, dims, preferred_element_type=F32)


def unit(values):
    average = jnp.mean(values, axis=0, keepdims=True)
    centered = values - average
    variance = jnp.mean(centered * centered, axis=0, keepdims=True)
    scale = lax.rsqrt(variance + EPS)
    return centered * scale, scale


def unit_back(normed, scale, incoming):
    return scale * (
        incoming
        - jnp.mean(incoming, axis=0, keepdims=True)
        - normed * jnp.mean(incoming * normed, axis=0, keepdims=True)
    )


def gated(projected, channels, group):
    gate = jax.nn.sigmoid(projected[2 * group * channels : (2 * group + 1) * channels])
    return gate * projected[(2 * group + 1) * channels : (2 * group + 2) * channels]


def taken(ref, rows, wide, *first):
    lanes = ref.shape[-1]
    chunks = [ref[(*first, k, rows, slice(None))] for k in range(ref.shape[-3])]
    return jnp.concatenate(chunks, axis=1)[:, :wide] if len(chunks) * lanes > wide else chunks[0]


def put(ref, rows, values, *first):
    lanes = ref.shape[-1]
    short = ref.shape[-3] * lanes - values.shape[1]
    if short > 0:
        values = jnp.concatenate([values, jnp.zeros((values.shape[0], short), F32)], axis=1)
    for k in range(ref.shape[-3]):
        ref[(*first, k, rows, slice(None))] = values[:, k * lanes : (k + 1) * lanes]


def looped(first, end, batch, compute):
    def step(block, carry):
        stores = [compute(block * batch + k) for k in range(batch)]
        for store in stores:
            store()
        return carry

    lax.fori_loop(first // batch, end // batch, step, 0)


def body(
    devices,
    slots,
    edge,
    channels,
    own_ref, low_ref, high_ref, cot_ref, mask_ref, w_in_ref, w_in_t_ref, w_out_ref, w_out_t_ref,
    update_ref, grad_ref, weights_ref,
    slabs, left, right, band, gates, saved, d_projected, tri, d_left, d_right, packed, arrived, spread,
    terms, landed, slab_send, slab_recv, pack_send, pack_recv, sum_send, sum_recv,
):
    half = slots // 2
    rows = edge * channels
    wide = slots * edge
    lanes = slabs.shape[2]
    folds = lanes // edge
    steps = devices.bit_length() - 1
    offsets = [d for d in range(-half, half + 1) if d != 0]
    me = lax.axis_index("row")

    def there(d):
        return jnp.logical_and(me + d >= 0, me + d < devices)

    partners = []
    for step in range(steps):
        bit = 1 << step
        partners.append(me + bit * (1 - 2 * lax.rem(me // bit, 2)))

    def greet(target):
        pl.semaphore_signal(
            barrier, inc=1, device_id={"row": target}, device_id_type=pl.DeviceIdType.MESH
        )

    barrier = pltpu.get_barrier_semaphore()
    for d in offsets:
        pl.when(there(d))(functools.partial(greet, me + d))
    for partner in partners:
        greet(partner)
    pl.semaphore_wait(barrier, steps + sum(there(d).astype(jnp.int32) for d in offsets))

    even = lax.rem(me, 2) == 0
    odd = jnp.logical_not(even)

    parts = 4
    size = rows // parts

    def part_of(p):
        return pl.ds(pl.multiple_of(p * size, size), size)

    def slab_copy(p, source, sem, target, landing):
        return pltpu.make_async_remote_copy(
            src_ref=source.at[part_of(p)],
            dst_ref=slabs.at[offsets.index(landing), part_of(p)],
            send_sem=slab_send.at[sem * parts + p],
            recv_sem=slab_recv.at[offsets.index(landing) * parts + p],
            device_id={"row": me + target},
            device_id_type=pl.DeviceIdType.MESH,
        )

    sends = [
        (there(1), (high_ref, 0, 1, -1)),
        (there(-1), (low_ref, 1, -1, 1)),
        (jnp.logical_and(even, there(2)), (high_ref, 2, 2, -2)),
        (jnp.logical_and(odd, there(-2)), (low_ref, 3, -2, 2)),
    ]
    relays = [
        (
            jnp.logical_and(even, jnp.logical_and(there(-1), there(1))),
            (slabs.at[offsets.index(-1)], 4, 1, -2),
        ),
        (jnp.logical_and(odd, there(1)), (slabs.at[offsets.index(1)], 5, -1, 2)),
    ]

    def pack_copy(d, landing):
        return pltpu.make_async_remote_copy(
            src_ref=packed.at[offsets.index(d)],
            dst_ref=arrived.at[offsets.index(landing)],
            send_sem=pack_send.at[offsets.index(d)],
            recv_sem=pack_recv.at[offsets.index(landing)],
            device_id={"row": me + d},
            device_id_type=pl.DeviceIdType.MESH,
        )

    for p in range(parts):
        for needed, route in sends:
            pl.when(needed)(lambda p=p, route=route: slab_copy(p, *route).start())

    w_in = w_in_ref[...]
    w_in_t = w_in_t_ref[...]
    w_out = w_out_ref[...]
    w_out_t = w_out_t_ref[...]
    mask = mask_ref[...]

    def at(i):
        return pl.ds(pl.multiple_of(i * channels, channels), channels)

    def four(i):
        return pl.ds(pl.multiple_of(i * 4 * channels, channels), 4 * channels)

    def project_own(i):
        normed, _ = unit(own_ref[at(i), :].astype(F32))
        projected = dot(w_in_t, normed.astype(BF16), NN)
        parts = []
        for group in range(2):
            low = 2 * group * channels
            parts.append(jax.nn.sigmoid(projected[low : low + channels]))
            parts.append(projected[low + channels : low + 2 * channels])
        gate = jax.nn.sigmoid(projected[4 * channels :])

        def store():
            put(left, at(i), (parts[0] * parts[1]).astype(BF16).astype(F32), half)
            put(right, at(i), (parts[2] * parts[3]).astype(BF16).astype(F32), half)
            saved[four(i), :] = jnp.concatenate(parts, axis=0)
            put(gates, at(i), gate)

        return store

    looped(0, edge, 2, project_own)

    def project_slab(p, d, relay):
        index = offsets.index(d)
        count = (slots - abs(d)) * edge
        skipped = max(0, -d - 1) * edge
        first = max(0, d) * edge

        def absent():
            slabs[index, part_of(p), :] = jnp.zeros((size, lanes), BF16)

        pl.when(there(d))(lambda: slab_copy(p, low_ref, 0, d, d).wait_recv())
        pl.when(jnp.logical_not(there(d)))(absent)
        if relay is not None:
            pl.when(relay[0])(lambda: slab_copy(p, *relay[1]).start())

        def placed(values):
            parts = [values[:, skipped : skipped + count]]
            if first > 0:
                parts = [jnp.zeros((channels, first), F32)] + parts
            tail = wide - first - count
            if tail > 0:
                parts = parts + [jnp.zeros((channels, tail), F32)]
            return jnp.concatenate(parts, axis=1)

        def project_far(block):
            picked = [block * 4 + k for k in range(4)]
            values = jnp.concatenate([slabs[index, at(i), :] for i in picked], axis=1)
            normed, _ = unit(values.astype(F32))
            projected = dot(w_in_t[: 4 * channels], normed.astype(BF16), NN)
            results = [gated(projected, channels, group).astype(BF16).astype(F32) for group in range(2)]

            def store():
                for result, ref in zip(results, (left, right)):
                    for k, i in enumerate(picked):
                        put(ref, at(i), placed(result[:, k * lanes : (k + 1) * lanes]), half + d)

            return store

        blocks = edge // 4 // parts
        looped(p * blocks, (p + 1) * blocks, 1, project_far)

    def same_chip(p, carry):
        pl.when(even)(lambda: project_slab(p, 1, None))
        pl.when(odd)(lambda: project_slab(p, -1, None))
        return carry

    lax.fori_loop(0, parts, same_chip, 0)

    def piece(block):
        return pl.ds(pl.multiple_of(block * 128, 128), 128)

    def cot_to_rows(block):
        values = cot_ref[:, piece(block)].astype(F32).T
        return lambda: put(d_left, piece(block), values)

    def cot_to_blocks(c):
        every = pl.ds(c, edge, stride=channels)
        turned = taken(d_left, every, wide).T
        values = jnp.concatenate([turned[w * edge : (w + 1) * edge] for w in range(slots)], axis=1)
        return lambda: put(d_right, every, values)

    looped(0, rows // 128, 2, cot_to_rows)
    looped(0, channels, 8, cot_to_blocks)
    def other_chip(p, carry):
        pl.when(even)(lambda: project_slab(p, -1, relays[0]))
        pl.when(odd)(lambda: project_slab(p, 1, relays[1]))
        project_slab(p, -2, None)
        project_slab(p, 2, None)
        return carry

    lax.fori_loop(0, parts, other_chip, 0)

    def triangle(c):
        every = pl.ds(c, edge, stride=channels)
        block = jnp.concatenate([taken(right, every, wide, v) for v in range(slots)], axis=0).astype(BF16)
        result = dot(taken(left, every, wide, half).astype(BF16), block, NT)

        def store():
            band[c] = block
            put(tri, every, result)

        return store

    looped(0, channels, 8, triangle)

    def middle(start, carry):
        total = carry
        d_tiles = []
        for fold in range(folds):
            i = start + fold * (edge // folds)
            normed, scale = unit(taken(tri, at(i), wide))
            normed_low = normed.astype(BF16)
            mixed = dot(w_out_t, normed_low, NN)
            gate = taken(gates, at(i), wide)
            put(gates, at(i), mask * gate * mixed)
            d_update = taken(d_right, at(i), wide) * mask
            d_mixed = (d_update * gate).astype(BF16)
            d_projected[i, 4 * channels :, :] = (d_update * mixed * gate * (1.0 - gate)).astype(BF16)
            total = total + dot(normed_low, d_mixed, NT)
            d_tri = unit_back(normed, scale, dot(w_out, d_mixed, NN)).astype(BF16).astype(F32)
            put(tri, at(i), d_tri)
            d_tiles.append(d_tri)
        for d in offsets:
            v = half + d
            packed[offsets.index(d), at(start), :] = jnp.concatenate(
                [tile[:, v * edge : (v + 1) * edge] for tile in d_tiles], axis=1
            ).astype(BF16)
        return total

    grad_out = lax.fori_loop(0, edge // folds, middle, jnp.zeros((channels, channels), F32))

    for d in offsets:
        pl.when(there(d))(lambda d=d: pack_copy(d, -d).start())

    def to_left(c):
        every = pl.ds(c, edge, stride=channels)
        result = dot(taken(tri, every, wide).astype(BF16), band[c], NN)
        return lambda: put(d_left, every, result)

    looped(0, channels, 8, to_left)

    def weigh(group, ref, joined_gate):
        def compute(block, carry):
            stores = []
            for i in (2 * block, 2 * block + 1):
                normed, _ = unit(own_ref[at(i), :].astype(F32))
                held = saved[four(i), :]
                gate = held[2 * group * channels : (2 * group + 1) * channels]
                value = held[(2 * group + 1) * channels : (2 * group + 2) * channels]
                to_value = taken(ref, at(i), wide) * mask * gate
                front = jnp.concatenate([to_value * value * (1.0 - gate), to_value], axis=0).astype(BF16)
                stores.append((i, front))
                if joined_gate:
                    front = jnp.concatenate([front, d_projected[i, 4 * channels :, :]], axis=0)
                carry = carry + dot(normed.astype(BF16), front, NT)
            for i, front in stores:
                d_projected[i, 2 * group * channels : (2 * group + 2) * channels, :] = front
            return carry

        width = (3 if joined_gate else 2) * channels
        return lax.fori_loop(0, edge // 2, compute, jnp.zeros((channels, width), F32))

    def summed(total, first, sem, beside):
        width = total.shape[1]
        for step, partner in enumerate(partners):
            terms[step, :, first : first + width] = total
            copy = pltpu.make_async_remote_copy(
                src_ref=terms.at[step, :, pl.ds(first, width)],
                dst_ref=landed.at[step, :, pl.ds(first, width)],
                send_sem=sum_send.at[sem + step],
                recv_sem=sum_recv.at[sem + step],
                device_id={"row": partner},
                device_id_type=pl.DeviceIdType.MESH,
            )
            copy.start()
            beside(step)
            copy.wait()
            total = total + landed[step, :, first : first + width]
        weights_ref[:, first : first + width] = total

    early = jnp.concatenate([weigh(0, d_left, True), grad_out], axis=1)

    def take_packs():
        for d in offsets:
            index = offsets.index(d)

            def absent(index=index):
                arrived[index] = jnp.zeros(arrived.shape[1:], BF16)

            pl.when(there(d))(lambda d=d: pack_copy(d, d).wait_recv())
            pl.when(jnp.logical_not(there(d)))(absent)
            spread[index] = arrived[index].astype(F32)

    def to_right(c):
        every = pl.ds(c, edge, stride=channels)
        folded = pl.ds(c, edge // folds, stride=channels)
        pieces = []
        sources = []
        for d in range(-half, half + 1):
            sources.append(taken(left, every, wide, half + d))
            if d == 0:
                pieces.append(taken(tri, every, wide)[:, half * edge : (half + 1) * edge])
            else:
                tile = spread[offsets.index(d), folded, :]
                for fold in range(folds):
                    pieces.append(tile[:, fold * edge : (fold + 1) * edge])
        d_tile = jnp.concatenate(pieces, axis=0).astype(BF16)
        source = jnp.concatenate(sources, axis=0).astype(BF16)
        result = dot(d_tile, source, TN)
        return lambda: put(d_right, every, result)

    def beside_early(step):
        if step == 0:
            take_packs()
        looped(channels // 4 * step // steps * 4, channels // 4 * (step + 1) // steps * 4, 4, to_right)

    summed(early, 0, 0, beside_early)
    late = weigh(1, d_right, False)

    def to_pair(i):
        normed, scale = unit(own_ref[at(i), :].astype(F32))
        result = unit_back(normed, scale, dot(w_in, d_projected[i], NN)).astype(BF16)

        def store():
            grad_ref[at(i), :] = result

        return store

    def update_to_rows(c):
        every = pl.ds(c, edge, stride=channels)
        values = taken(gates, every, wide)
        values = jnp.concatenate([values[:, w * edge : (w + 1) * edge] for w in range(slots)], axis=0).T
        return lambda: put(tri, every, values)

    def update_to_tiles(block):
        values = taken(tri, piece(block), wide).T.astype(BF16)

        def store():
            update_ref[:, piece(block)] = values

        return store

    def beside_late(step):
        middle_step = steps // 2
        if step < middle_step:
            blocks = channels // 4
            looped(blocks * step // middle_step * 4, blocks * (step + 1) // middle_step * 4, 4, update_to_rows)
        else:
            blocks, step_now, step_count = rows // 256, step - middle_step, steps - middle_step
            looped(blocks * step_now // step_count * 2, blocks * (step_now + 1) // step_count * 2, 2, update_to_tiles)
        looped(edge // 2 * step // steps * 2, edge // 2 * (step + 1) // steps * 2, 2, to_pair)

    summed(late, 4 * channels, steps, beside_late)

    for p in range(parts):
        for needed, route in sends + relays:
            pl.when(needed)(lambda p=p, route=route: slab_copy(p, *route).wait_send())
    for d in offsets:
        pl.when(there(d))(lambda d=d: pack_copy(d, -d).wait_send())


def local(pair, kept, w_in, w_out, cotangent):
    slots, edge = pair.shape[1], pair.shape[2]
    channels = w_in.shape[0]
    half = slots // 2
    rows, wide = edge * channels, slots * edge
    lanes = wide - edge
    chunks = -(-wide // lanes)
    devices = lax.axis_size("row")
    steps = devices.bit_length() - 1

    def to_columns(tiles):
        return jnp.transpose(tiles, (1, 3, 0, 2)).reshape(rows, wide)

    def from_columns(columns):
        tiles = columns.reshape(edge, channels, slots, edge)
        return jnp.transpose(tiles, (2, 0, 3, 1)).reshape(pair.shape)

    tiles = pair[0].reshape(slots, edge, edge, channels)
    own = to_columns(tiles * kept[0].astype(BF16)[:, None, None, None])
    cot = cotangent[0].reshape(wide, rows)
    mask = jnp.repeat(kept[0].astype(F32), edge)[None, :]
    low, high = own[:, :lanes], own[:, edge:]

    whole = pl.BlockSpec(memory_space=pltpu.VMEM)
    far = 2 * half
    update, grad, weights = pl.pallas_call(
        functools.partial(body, devices, slots, edge, channels),
        out_shape=(
            jax.ShapeDtypeStruct((wide, rows), BF16),
            jax.ShapeDtypeStruct((rows, wide), BF16),
            jax.ShapeDtypeStruct((channels, 6 * channels), F32),
        ),
        in_specs=[whole] * 9,
        out_specs=(whole, whole, whole),
        scratch_shapes=[
            pltpu.VMEM((far, rows, lanes), BF16),
            pltpu.VMEM((slots, chunks, rows, lanes), F32),
            pltpu.VMEM((slots, chunks, rows, lanes), F32),
            pltpu.VMEM((channels, wide, wide), BF16),
            pltpu.VMEM((chunks, rows, lanes), F32),
            pltpu.VMEM((4 * rows, wide), F32),
            pltpu.VMEM((edge, 5 * channels, wide), BF16),
            pltpu.VMEM((chunks, rows, lanes), F32),
            pltpu.VMEM((chunks, rows, lanes), F32),
            pltpu.VMEM((chunks, rows, lanes), F32),
            pltpu.VMEM((far, rows * edge // lanes, lanes), BF16),
            pltpu.VMEM((far, rows * edge // lanes, lanes), BF16),
            pltpu.VMEM((far, rows * edge // lanes, lanes), F32),
            pltpu.VMEM((steps, channels, 6 * channels), F32),
            pltpu.VMEM((steps, channels, 6 * channels), F32),
            pltpu.SemaphoreType.DMA((4 * (far + 2),)),
            pltpu.SemaphoreType.DMA((4 * far,)),
            pltpu.SemaphoreType.DMA((far,)),
            pltpu.SemaphoreType.DMA((far,)),
            pltpu.SemaphoreType.DMA((2 * steps,)),
            pltpu.SemaphoreType.DMA((2 * steps,)),
        ],
        compiler_params=pltpu.CompilerParams(
            collective_id=0, has_side_effects=True, vmem_limit_bytes=63 * 1024 * 1024
        ),
    )(own, low, high, cot, mask, w_in, w_in.T, w_out, w_out.T)
    first, gate, out, second = jnp.split(
        weights, [2 * channels, 3 * channels, 4 * channels], axis=1
    )
    grad_w_in = jnp.concatenate([first, second, gate], axis=1)
    grad_w_out = out
    return (update.reshape(pair.shape), from_columns(grad), grad_w_in, grad_w_out)


def solution(mesh):
    tiled = P(("grp", "row"), None, None, None)
    return jax.shard_map(
        local,
        mesh=mesh,
        in_specs=(tiled, P(("grp", "row"), None), P(), P(), tiled),
        out_specs=(tiled, tiled, P("grp", None), P("grp", None)),
        check_vma=False,
    )
```
